32 devices in a mesh: member: 2 (over y), comp: 4 (over z), lev: 4 (over x, core).
Axes of the slice: x: 2, y: 2, z: 4, core: 2. Of those that a mesh axis runs over, the one named last changes fastest.
Arguments:
- atm_state: float32 [144, 64, 512], P('member', 'comp', 'lev'), parts along dimension 0, may hold values from -6 to 6
- ocean_state: float32 [120, 64, 1024], P('member', 'comp', 'lev'), parts along dimension 0, may hold values from -6 to 6
- flux_prev: bfloat16 [16, 64, 512], P('member', 'comp', 'lev'), parts along dimension 0, may hold values from -6 to 6
- pair_offset: int32 [2048], P(('comp', 'lev')), may hold values from 0 to 8, as said below
- pair_tile: int32 [2048], P(('comp', 'lev')), may hold values from 0 to 15
- pair_weight: bfloat16 [2048, 128, 256], P(('comp', 'lev')), may hold values from 0.0019989014 to 0.019897461
- atm_mix: float32 [72, 72], replicated, may hold values from 0 to 1
- ocean_mix: float32 [60, 60], replicated, may hold values from 0 to 1
- exchange_response_matrix: float32 [8, 72], replicated, may hold values from -0.75 to 0.75
- exchange_factor_array: float32 [8], replicated, may hold values from 0.5 to 2
- depth_profile: float32 [60, 8], replicated, may hold values from -2 to 2
- sea_mask: int32 [64, 1024], P('comp', 'lev'), may hold values 0 or 1
Outputs:
- atm_next: float32 [144, 64, 512], P('member', 'comp', 'lev'), parts along dimension 0
- ocean_next: float32 [120, 64, 1024], P('member', 'comp', 'lev'), parts along dimension 0
- flux_next: bfloat16 [16, 64, 512], P('member', 'comp', 'lev'), parts along dimension 0
The draws below stay inside these ranges and needn't reach their ends.
There are 2 independent parts, one for each index of `member`. The reference program is written for one: setup_inputs(seed, part) draws one part's arguments, and reference() takes and returns one part's arrays. A program takes and returns all parts, laid end to end along the dimension named above; an argument that names none is the same for every part. Nothing has to cross between parts.
Inputs may be any that keep to these rules, and one draw needn't show every extreme that they name: `pair_offset`: among the 128 pairs of one block, offset 4 (the block itself) appears 128 / 4 times, each of 1, 3, 5, 7 * 128 / 8 times and each of 0, 2, 6, 8 * 128 / 16 times; offset d stands for the block d // 3 - 1 rows and d % 3 - 1 columns of blocks away.
All inputs are finite; a program needn't handle non-finite values. No bound on the sum of `sea_mask` on one device may be relied on, other than what follows from the above.
Results may differ from the reference program's by a relative error of at most 0.0049.
Values may be sent and summed in bfloat16 or wider, within the bound.
A program may use at most 64 MiB of HBM per device.

```python
import math
import jax
import jax.numpy as jnp
from jax import lax

AIR_VERTICAL_N = 72
KO = 60
FLUX = 8
AIR_LATITUDE_N = 16
AIR_TILE_CELLS = 128
OY = 16
OX = 256
PAIRS_TILE = 8
ASTEPS = 4
OSTEPS = 4
PANEL_TOTAL = 16
PAIRS_DEV = 128
NPAIRS = 2048
NAY = 64
NAX = 512
NOY = 64
NOX = 1024
N_COMP = 4
N_LEV = 4


def mixing(key, order, diagonal_part, spread_part):
    noise = jax.random.uniform(key, (order, order), jnp.float32, 0.0, 2.0)
    return diagonal_part * jnp.eye(order, dtype=jnp.float32) + spread_part * noise / order


def draw_atm_mix(key, part):
    key = jax.random.fold_in(key, 11)
    return mixing(key, AIR_VERTICAL_N, 0.55, 0.45)


def draw_ocean_mix(key, part):
    key = jax.random.fold_in(key, 23)
    return mixing(key, KO, 0.65, 0.5)


def draw_ocean_state(key, part):
    key = jax.random.fold_in(key, 41)
    sign_key, amplitude_key = jax.random.split(key)
    row_index = jnp.arange(NOY, dtype=jnp.int32)[:, None]
    col_index = jnp.arange(NOX, dtype=jnp.int32)[None, :]
    parity = ((row_index + col_index) % 2).astype(jnp.float32) * 2.0 - 1.0
    overall = jax.random.randint(sign_key, (), 0, 2).astype(jnp.float32) * 2.0 - 1.0
    amplitude = 4.5 + 0.75 * jnp.clip(jax.random.normal(amplitude_key, (KO, NOY, NOX), jnp.float32), -2.0, 2.0)
    return (overall * amplitude * parity[None]).astype(jnp.float32)


def draw_pair_offset(key, part):
    key = jax.random.fold_in(key, 37)
    share = PAIRS_DEV // 16
    weights_each = [1, 2, 1, 2, 4, 2, 1, 2, 1]
    pieces = [jnp.full((share * weights_each[offset_index],), offset_index, jnp.int32) for offset_index in range(9)]
    base = jnp.concatenate(pieces)
    block_keys = jax.random.split(key, PANEL_TOTAL)
    shuffled = jax.vmap(lambda block_key: jax.random.permutation(block_key, base))(block_keys)
    return shuffled.reshape(NPAIRS).astype(jnp.int32)


def touch_ends(array, stream_key, smallest, top_value):
    extent = array.shape
    place = [jax.random.randint(jax.random.fold_in(stream_key, axis), (), 0, extent[axis]) for axis in range(len(extent))]
    array = array.at[tuple(place)].set(smallest)
    longest = extent.index(max(extent))
    place[longest] = (place[longest] + 1) % extent[longest]
    return array.at[tuple(place)].set(top_value)


def levels(stream_key, shape, cuts, least, high):
    level = 1.0
    for axis_at, parts in cuts:
        steps = jax.random.uniform(jax.random.fold_in(jax.random.fold_in(stream_key, 6), axis_at), (parts,), jnp.float32, least / len(cuts), high / len(cuts))
        level = level * jnp.repeat(jnp.exp(steps), shape[axis_at] // parts).reshape((-1,) + (1,) * (len(shape) - 1 - axis_at))
    return level


def normal_values(own_key, dims, deviation, limit, shards=(), kind=jnp.bfloat16):
    gain = levels(own_key, dims, shards, -0.22, 0.18) if shards else 1.0
    entries = jax.random.normal(own_key, dims, jnp.float32) * deviation * gain
    return jnp.minimum(jnp.maximum(entries, -limit), limit).astype(kind)


def setup_inputs(seed: int = 0, part: int = 0) -> dict:
    streams_of = jax.random.split(jax.random.key(seed), 13)
    part_keys = jax.random.split(jax.random.fold_in(streams_of[12], part), 13)
    return {
        "atm_state": normal_values(part_keys[0], (AIR_VERTICAL_N, NAY, NAX), 1.0, 6.0, ((1, 4), (2, 4)), jnp.float32),
        "ocean_state": draw_ocean_state(jax.random.fold_in(jax.random.fold_in(streams_of[12], part), 71), part),
        "flux_prev": normal_values(part_keys[2], (FLUX, NAY, NAX), 1.0, 6.0, ((1, 4), (2, 4))),
        "pair_offset": draw_pair_offset(jax.random.fold_in(streams_of[12], 71), part),
        "pair_tile": touch_ends(jax.random.randint(streams_of[4], (NPAIRS,), 0, OY), jax.random.fold_in(streams_of[4], 1), 0, OY - 1).astype(jnp.int32),
        "pair_weight": jnp.clip(jnp.exp(math.log(0.019897461) - 2.2979944 * jax.random.uniform(streams_of[5], (NPAIRS, AIR_TILE_CELLS, OX), jnp.float32) ** levels(streams_of[5], (NPAIRS, AIR_TILE_CELLS, OX), ((0, 16),), -0.2, 0.2)), 0.0019989014, 0.019897461).astype(jnp.bfloat16),
        "atm_mix": draw_atm_mix(jax.random.fold_in(streams_of[12], 71), part),
        "ocean_mix": draw_ocean_mix(jax.random.fold_in(streams_of[12], 71), part),
        "exchange_response_matrix": normal_values(streams_of[8], (FLUX, AIR_VERTICAL_N), AIR_VERTICAL_N ** -0.5, 0.75, (), jnp.float32),
        "exchange_factor_array": jnp.clip(jax.random.uniform(streams_of[9], (FLUX,), jnp.float32, 0.5, 2.0), 0.5, 2.0),
        "depth_profile": normal_values(streams_of[10], (KO, FLUX), FLUX ** -0.5, 2.0, (), jnp.float32),
        "sea_mask": touch_ends((jax.random.randint(streams_of[11], (NOY, NOX), 0, 10) < 7).astype(jnp.int32), jax.random.fold_in(streams_of[11], 1), 0, 1),
    }


atmos_diffusion = 0.24
ocean_diffusion = 0.24
interface_linkage = 0.5


def laplace(field):
    padded = jnp.pad(field, ((0, 0), (1, 1), (1, 1)))
    return padded[:, 2:, 1:-1] + padded[:, :-2, 1:-1] + padded[:, 1:-1, 2:] + padded[:, 1:-1, :-2] - 4.0 * field


def column_mix(matrix, field):
    return jnp.einsum('kj,jyx->kyx', matrix, field, precision=lax.Precision.HIGHEST)


def reflect(index, count):
    return jnp.where(index < 0, -index, jnp.where(index > count - 1, 2 * (count - 1) - index, index)).astype(jnp.int32)


def to_tiles(field, rows, cols):
    chan = field.shape[0]
    split = field.reshape(chan, N_COMP, rows, N_LEV, cols)
    return split.transpose(1, 3, 2, 0, 4).reshape(N_COMP * N_LEV * rows, chan, cols)


def collected_panels(tiles, rows, cols):
    chan = tiles.shape[1]
    split = tiles.reshape(N_COMP, N_LEV, rows, chan, cols)
    return split.transpose(3, 0, 2, 1, 4).reshape(chan, N_COMP * rows, N_LEV * cols)


def regrid_block(pieces):
    block_flux, block_weight, block_slot = pieces
    products = jnp.einsum('yca,ypao->ypco', block_flux.astype(jnp.float32), block_weight.astype(jnp.float32),
                          precision=lax.Precision.HIGHEST).reshape(PAIRS_DEV, FLUX * OX)
    select = (jnp.arange(9 * OY, dtype=jnp.int32)[:, None] == block_slot[None, :]).astype(jnp.float32)
    return jnp.dot(select, products, precision=lax.Precision.HIGHEST).astype(jnp.bfloat16)


def surface_block(pieces):
    block_rows, block_weight = pieces
    stacked = jnp.stack([block_rows, jnp.ones_like(block_rows)], axis=2).astype(jnp.float32)
    return jnp.einsum('ypjo,ypao->jya', stacked, block_weight.astype(jnp.float32), precision=lax.Precision.HIGHEST)


def reference(atm_state, ocean_state, flux_prev, pair_offset, pair_tile, pair_weight, atm_mix, ocean_mix,
              exchange_response_matrix, exchange_factor_array, depth_profile, sea_mask):
    block_ids = jnp.arange(NPAIRS, dtype=jnp.int32) // PAIRS_DEV
    row_block = block_ids // N_LEV
    col_block = block_ids % N_LEV
    dest_row = reflect(row_block + pair_offset // 3 - 1, N_COMP)
    dest_col = reflect(col_block + pair_offset % 3 - 1, N_LEV)
    near_index = (dest_row - row_block + 1) * 3 + (dest_col - col_block + 1)
    slot = (near_index * OY + pair_tile).astype(jnp.int32)
    target = ((dest_row * N_LEV + dest_col) * OY + pair_tile).astype(jnp.int32)

    weights = pair_weight.reshape(PANEL_TOTAL, AIR_LATITUDE_N, PAIRS_TILE, AIR_TILE_CELLS, OX)
    flux_tiles = to_tiles(flux_prev, AIR_LATITUDE_N, AIR_TILE_CELLS).reshape(PANEL_TOTAL, AIR_LATITUDE_N, FLUX, AIR_TILE_CELLS)
    partial_value = lax.map(regrid_block, (flux_tiles, weights, slot.reshape(PANEL_TOTAL, PAIRS_DEV)))
    blocks_all = jnp.arange(PANEL_TOTAL, dtype=jnp.int32)
    slots_all = jnp.arange(9 * OY, dtype=jnp.int32)
    near_all = slots_all // OY
    slot_row = reflect((blocks_all // N_LEV)[:, None] + (near_all // 3 - 1)[None, :], N_COMP)
    slot_col = reflect((blocks_all % N_LEV)[:, None] + (near_all % 3 - 1)[None, :], N_LEV)
    slot_target = ((slot_row * N_LEV + slot_col) * OY + (slots_all % OY)[None, :]).astype(jnp.int32)
    received = jax.ops.segment_sum(partial_value.reshape(PANEL_TOTAL * 9 * OY, FLUX * OX).astype(jnp.float32),
                                   slot_target.reshape(PANEL_TOTAL * 9 * OY), num_segments=PANEL_TOTAL * OY)
    received = collected_panels(received.reshape(PANEL_TOTAL * OY, FLUX, OX), OY, OX)
    forcing = jnp.einsum('kc,cyx->kyx', depth_profile, received, precision=lax.Precision.HIGHEST)
    wet = sea_mask.astype(jnp.float32)
    ocean = ocean_state
    for step in range(OSTEPS):
        ocean = wet * (column_mix(ocean_mix, ocean + ocean_diffusion * laplace(ocean)) + forcing)
    surface = to_tiles(ocean_state[0:1].astype(jnp.bfloat16), OY, OX)[:, 0, :]
    rows = surface[target].reshape(PANEL_TOTAL, AIR_LATITUDE_N, PAIRS_TILE, OX)
    panel_totals = lax.map(surface_block, (rows, weights))
    linkage_fraction = panel_totals[:, 0] / panel_totals[:, 1]
    ocean_skin_heat_for_air = collected_panels(linkage_fraction.reshape(PANEL_TOTAL * AIR_LATITUDE_N, 1, AIR_TILE_CELLS), AIR_LATITUDE_N, AIR_TILE_CELLS)[0]
    atmos = atm_state
    exchange_total = jnp.zeros((FLUX, NAY, NAX), jnp.float32)
    for step in range(ASTEPS):
        blended_air_profiles = column_mix(atm_mix, atmos + atmos_diffusion * laplace(atmos))
        thermal_difference = ocean_skin_heat_for_air - blended_air_profiles[AIR_VERTICAL_N - 1]
        blended_air_profiles = blended_air_profiles.at[AIR_VERTICAL_N - 1].add(interface_linkage * thermal_difference)
        exchange_total = exchange_total + jnp.einsum('jr,rip->jip', exchange_response_matrix, blended_air_profiles, precision=lax.Precision.HIGHEST) + exchange_factor_array[:, None, None] * thermal_difference[None]
        atmos = blended_air_profiles
    return atmos, ocean, (exchange_total / ASTEPS).astype(jnp.bfloat16)
```

```python
import jax
import jax.numpy as jnp
from jax import lax
from jax.experimental import pallas as pl
from jax.experimental.pallas import tpu as pltpu
from jax.sharding import PartitionSpec as P

STEPS = 4
RATE = 0.24
LINK = 0.5
BF16 = jnp.bfloat16
F32 = jnp.float32
MESH = pl.DeviceIdType.MESH
NEAR = [(n // 3 - 1, n % 3 - 1) for n in range(9)]
SIDES = [(-1, 0), (1, 0), (0, -1), (0, 1)]


def halves(x):
    hi = x.astype(BF16)
    return hi, (x - hi.astype(F32)).astype(BF16)


def split_outside(x):
    hi = lax.reduce_precision(x, 8, 7)
    return hi.astype(BF16), (x - hi).astype(BF16)


def padded(x, rows, cols):
    return jnp.pad(x, ((0, rows - x.shape[0]), (0, cols - x.shape[1])))


def reflect(index, count):
    return jnp.where(
        index < 0, -index, jnp.where(index > count - 1, 2 * (count - 1) - index, index)
    )


def make_kernel(dims):
    rows, per_tile, chan, cells_a, cells_o, last, counts = dims
    pairs = rows * per_tile

    def kernel(
        ocean_in, atm_in, flux_ref, weight_in, surf_in, slot_row, slot_col, omat, amat, coef, wet,
        ocean_out, atm_out, flux_out,
        ocean, atm, wbuf, prod, part, precv, surf, gathered, forced, ou, au, sst,
        orow, ocol, oedge, arow, acol, aedge,
        in_sem, w_sem, surf_send, surf_recv, part_send, part_recv,
        o_send, o_recv, a_send, a_recv,
    ):
        ci = lax.axis_index("comp")
        li = lax.axis_index("lev")
        comp_count, lev_count = counts

        def there(di, dj):
            ok = None
            for delta, index, count in ((di, ci, comp_count), (dj, li, lev_count)):
                if delta == -1:
                    one = index > 0
                elif delta == 1:
                    one = index < count - 1
                else:
                    continue
                ok = one if ok is None else jnp.logical_and(ok, one)
            return ok

        def device(di, dj):
            return {
                "comp": jnp.clip(ci + di, 0, comp_count - 1),
                "lev": jnp.clip(li + dj, 0, lev_count - 1),
            }

        load_ocean = pltpu.make_async_copy(ocean_in, ocean, in_sem.at[0])
        load_atm = pltpu.make_async_copy(atm_in, atm, in_sem.at[1])
        load_ocean.start()
        load_atm.start()

        def load_weight(y):
            return pltpu.make_async_copy(weight_in.at[y], wbuf.at[y], w_sem.at[y])

        def start_weight(y, carry):
            load_weight(y).start()
            return carry

        lax.fori_loop(0, rows, start_weight, 0)

        surf[4] = surf_in[...]
        for n, (di, dj) in enumerate(NEAR):
            if n != 4:
                @pl.when(jnp.logical_not(there(di, dj)))
                def _():
                    surf[n] = jnp.zeros_like(surf_in)
        for side, (di, dj) in enumerate(SIDES):
            @pl.when(jnp.logical_not(there(di, dj)))
            def _():
                for rbuf, cbuf in ((orow, ocol), (arow, acol)):
                    buf = rbuf if side < 2 else cbuf
                    for s in range(STEPS):
                        buf[s, side % 2] = jnp.zeros(buf.shape[2:], F32)

        barrier = pltpu.get_barrier_semaphore()
        for n, (di, dj) in enumerate(NEAR):
            if n != 4:
                @pl.when(there(di, dj))
                def _():
                    pl.semaphore_signal(
                        barrier, inc=1, device_id=device(di, dj), device_id_type=MESH
                    )
        tall = 1 + (ci > 0).astype(jnp.int32) + (ci < comp_count - 1).astype(jnp.int32)
        wide = 1 + (li > 0).astype(jnp.int32) + (li < lev_count - 1).astype(jnp.int32)

        def remote(src, dst, send, recv, di, dj):
            return pltpu.make_async_remote_copy(
                src_ref=src, dst_ref=dst, send_sem=send, recv_sem=recv,
                device_id=device(di, dj), device_id_type=MESH,
            )

        def surf_copy(n):
            return remote(
                surf.at[4], surf.at[8 - n], surf_send.at[n], surf_recv.at[n], *NEAR[n]
            )

        def part_copy(n):
            return remote(
                part.at[n], precv.at[n], part_send.at[n], part_recv.at[n], *NEAR[n]
            )

        def side_copy(state, rbuf, cbuf, edge, send, recv, s, side):
            if side < 2:
                src = state.at[0 if side == 0 else rows - 1]
                dst = rbuf.at[s, 1 - side]
            else:
                src = edge.at[side - 2]
                dst = cbuf.at[s, 3 - side]
            return remote(
                src, dst, send.at[s, side], recv.at[s, side], *SIDES[side]
            )

        ocean_parts = (ocean, orow, ocol, oedge, o_send, o_recv)
        atm_parts = (atm, arow, acol, aedge, a_send, a_recv)

        def start_sides(parts, s):
            for side, (di, dj) in enumerate(SIDES):
                @pl.when(there(di, dj))
                def _():
                    side_copy(*parts, s, side).start()

        def wait_sent(parts, s):
            for side, (di, dj) in enumerate(SIDES):
                @pl.when(there(di, dj))
                def _():
                    side_copy(*parts, s, side).wait_send()

        def wait_sides(parts, s):
            for side, (di, dj) in enumerate(SIDES):
                @pl.when(there(-di, -dj))
                def _():
                    side_copy(*parts, s, side).wait_recv()

        def pack(slabs, edge):
            depth = edge.shape[1]
            lane = lax.broadcasted_iota(jnp.int32, (depth, 128), 1)
            left = jnp.zeros((depth, 128), F32)
            right = jnp.zeros((depth, 128), F32)
            for r in range(rows):
                first, final = slabs(r)
                left = jnp.where(lane == r, pltpu.roll(first, r, 1) if r else first, left)
                right = jnp.where(lane == r, pltpu.roll(final, r + 1, 1), right)
            edge[0] = left
            edge[1] = right

        def ends(state):
            width = state.shape[2]
            return lambda r: (state[r, :, 0:128], state[r, :, width - 128:width])

        load_ocean.wait()
        pack(ends(ocean), oedge)
        load_atm.wait()
        pack(ends(atm), aedge)
        pl.semaphore_wait(barrier, tall * wide - 1)

        for n, (di, dj) in enumerate(NEAR):
            if n != 4:
                @pl.when(there(di, dj))
                def _():
                    surf_copy(n).start()
        start_sides(atm_parts, 0)
        start_sides(ocean_parts, 0)

        which = lax.broadcasted_iota(jnp.int32, (chan * per_tile, cells_a), 0) % per_tile

        def multiply(y, carry):
            load_weight(y).wait()
            flux = flux_ref[y]
            left = jnp.concatenate(
                [jnp.where(which == p, flux, 0.0).astype(BF16) for p in range(per_tile)], axis=1
            )
            out = jnp.dot(left, wbuf[y], preferred_element_type=F32)
            at = pl.ds(pl.multiple_of(y * per_tile, per_tile), per_tile)
            for c in range(chan):
                prod[c, at, :] = out[c * per_tile:(c + 1) * per_tile]
            return carry

        lax.fori_loop(0, rows, multiply, 0)

        slots = 9 * rows
        pick = (
            lax.broadcasted_iota(jnp.int32, (slots, pairs), 0) == slot_row[...]
        ).astype(F32).astype(BF16)
        pick = jnp.concatenate([pick, pick], axis=1)
        for c in range(chan):
            hi, lo = halves(prod[c])
            sums = jnp.dot(
                pick, jnp.concatenate([hi, lo], axis=0), preferred_element_type=F32
            ).astype(BF16)
            for n in range(9):
                part[n, c] = sums[n * rows:(n + 1) * rows]
        for n, (di, dj) in enumerate(NEAR):
            if n != 4:
                @pl.when(there(di, dj))
                def _():
                    part_copy(n).start()

        for n, (di, dj) in enumerate(NEAR):
            if n != 4:
                @pl.when(there(-di, -dj))
                def _():
                    surf_copy(n).wait_recv()
        group = 16
        wanted = (
            lax.broadcasted_iota(jnp.int32, (rows * group, slots), 1) == slot_col[...]
        ).astype(F32).astype(BF16)
        found = jnp.dot(wanted, surf[...].reshape(slots, cells_o), preferred_element_type=F32)
        spare = lax.broadcasted_iota(jnp.int32, (rows * group, cells_o), 0) % group >= per_tile
        gathered[...] = jnp.where(spare, 1.0, found).astype(BF16).reshape(rows, group, cells_o)
        line = lax.broadcasted_iota(jnp.int32, (8, cells_a), 0)

        def regrid(y, carry):
            out = lax.dot_general(
                gathered[y], wbuf[y], (((1,), (1,)), ((), ())), preferred_element_type=F32
            )
            num = jnp.zeros((8, cells_a), F32)
            den = jnp.zeros((8, cells_a), F32)
            for p in range(per_tile):
                cols = slice(p * cells_a, (p + 1) * cells_a)
                num = num + jnp.where(line == p, out[0:8, cols], 0.0)
                den = den + out[8:16, cols]
            total = jnp.sum(num, axis=0, keepdims=True)
            sst[y] = jnp.broadcast_to(total, (8, cells_a)) / den
            return carry

        lax.fori_loop(0, rows, regrid, 0)
        flux_out[...] = jnp.zeros_like(flux_out)

        def stencil(parts, s, r):
            state, rbuf, cbuf = parts[0], parts[1], parts[2]
            depth, width = state.shape[1], state.shape[2]
            lane = lax.broadcasted_iota(jnp.int32, (depth, 128), 1)
            x = state[r]
            up = rbuf[s, 0] if r == 0 else state[r - 1]
            down = rbuf[s, 1] if r == rows - 1 else state[r + 1]
            west = pltpu.roll(x, 1, 1)
            east = pltpu.roll(x, width - 1, 1)
            from_west = cbuf[s, 0]
            if r:
                from_west = pltpu.roll(from_west, 128 - r, 1)
            from_east = pltpu.roll(cbuf[s, 1], 127 - r, 1)
            west_end = jnp.where(lane == 0, from_west, west[:, 0:128])
            east_end = jnp.where(lane == 127, from_east, east[:, width - 128:width])
            if width > 128:
                west_end = jnp.concatenate([west_end, west[:, 128:]], axis=1)
                east_end = jnp.concatenate([east[:, 0:width - 128], east_end], axis=1)
            return (1.0 - 4.0 * RATE) * x + RATE * ((up + down) + (west_end + east_end))

        def step(s, carry):
            wait_sides(atm_parts, s)
            for r in range(rows):
                hi, lo = halves(stencil(atm_parts, s, r))
                au[r] = jnp.concatenate([hi, hi, lo], axis=0)
            wait_sent(atm_parts, s)
            depth = atm.shape[1]
            level = lax.broadcasted_iota(jnp.int32, (depth, cells_a), 0)
            for r in range(rows):
                mixed = jnp.dot(amat[...], au[r], preferred_element_type=F32)
                gap = sst[r, 0:1] - mixed[last:last + 1]
                flux_out[r] += mixed[last + 1:last + 1 + chan] + coef[...] * gap
                atm[r] = mixed + jnp.where(level == last, LINK * gap, 0.0)

            @pl.when(s < STEPS - 1)
            def _():
                pack(ends(atm), aedge)
                start_sides(atm_parts, s + 1)

            @pl.when(s == 0)
            def _():
                total = part[4].astype(F32).reshape(chan * rows, cells_o)
                prod[0, 0:chan * rows] = total
                for n, (di, dj) in enumerate(NEAR):
                    if n != 4:
                        @pl.when(there(-di, -dj))
                        def _():
                            part_copy(n).wait_recv()
                            prod[0, 0:chan * rows] += precv[n].astype(F32).reshape(
                                chan * rows, cells_o
                            )
                size = 4 * chan
                to = lax.broadcasted_iota(jnp.int32, (rows * size, chan * rows), 0)
                source = lax.broadcasted_iota(jnp.int32, (rows * size, chan * rows), 1)
                place = to % size
                turn = (
                    jnp.logical_and(
                        source == (place % chan) * rows + to // size, place < 3 * chan
                    )
                ).astype(F32).astype(BF16)
                hi, lo = halves(prod[0, 0:chan * rows])
                laid = jnp.dot(
                    jnp.concatenate([turn, turn], axis=1),
                    jnp.concatenate([hi, lo], axis=0),
                    preferred_element_type=F32,
                )
                high = laid.astype(BF16).astype(F32)
                at = lax.broadcasted_iota(jnp.int32, laid.shape, 0) % size
                both = jnp.where(at < 2 * chan, high, laid - high).astype(BF16)
                both = both.reshape(rows, size, cells_o)
                mixing = 3 * ocean.shape[1]
                for r in range(rows):
                    ou[r, mixing:mixing + size] = both[r]

            wait_sides(ocean_parts, s)
            deep = ocean.shape[1]
            for r in range(rows):
                hi, lo = halves(stencil(ocean_parts, s, r))
                ou[r, 0:3 * deep] = jnp.concatenate([hi, hi, lo], axis=0)
            wait_sent(ocean_parts, s)
            for r in range(rows):
                ocean[r] = wet[r:r + 1] * jnp.dot(
                    omat[...], ou[r], preferred_element_type=F32
                )

            @pl.when(s < STEPS - 1)
            def _():
                pack(ends(ocean), oedge)
                start_sides(ocean_parts, s + 1)

            return carry

        lax.fori_loop(0, STEPS, step, 0)

        save_ocean = pltpu.make_async_copy(ocean, ocean_out, in_sem.at[0])
        save_atm = pltpu.make_async_copy(atm, atm_out, in_sem.at[1])
        save_ocean.start()
        save_atm.start()
        for n, (di, dj) in enumerate(NEAR):
            if n != 4:
                @pl.when(there(di, dj))
                def _():
                    surf_copy(n).wait_send()
                    part_copy(n).wait_send()
        save_ocean.wait()
        save_atm.wait()

    return kernel


def body(
    atm_state,
    ocean_state,
    flux_prev,
    pair_offset,
    pair_tile,
    pair_weight,
    atm_mix,
    ocean_mix,
    exchange_response_matrix,
    exchange_factor_array,
    depth_profile,
    sea_mask,
):
    comp_count = lax.axis_size("comp")
    lev_count = lax.axis_size("lev")
    row_block = lax.axis_index("comp")
    col_block = lax.axis_index("lev")
    pairs, cells_a, cells_o = pair_weight.shape
    air, rows = atm_state.shape[:2]
    sea = ocean_state.shape[0]
    chan = flux_prev.shape[0]
    per_tile = pairs // rows
    deep = (sea + 15) // 16 * 16
    high = (air + chan + 15) // 16 * 16

    dest_row = reflect(row_block + pair_offset // 3 - 1, comp_count)
    dest_col = reflect(col_block + pair_offset % 3 - 1, lev_count)
    slot = ((dest_row - row_block + 1) * 3 + (dest_col - col_block + 1)) * rows + pair_tile
    slot_col = jnp.pad(
        slot.reshape(rows, per_tile), ((0, 0), (0, 16 - per_tile)), constant_values=-1
    ).reshape(rows * 16, 1)

    ocean_t = jnp.pad(ocean_state.transpose(1, 0, 2), ((0, 0), (0, deep - sea), (0, 0)))
    atm_t = jnp.pad(atm_state.transpose(1, 0, 2), ((0, 0), (0, high - air), (0, 0)))
    flux_t = jnp.repeat(flux_prev.transpose(1, 0, 2), per_tile, axis=1)
    surface = ocean_state[0].astype(BF16)

    omix_hi, omix_lo = split_outside(padded(ocean_mix, deep, deep))
    depth_hi, depth_lo = split_outside(padded(depth_profile, deep, chan))
    omat = jnp.concatenate(
        [omix_hi, omix_lo, omix_hi, depth_hi, depth_lo, depth_hi, jnp.zeros_like(depth_hi)], axis=1
    )
    response = jnp.dot(exchange_response_matrix, atm_mix, precision=lax.Precision.HIGHEST)
    amix_hi, amix_lo = split_outside(
        padded(jnp.concatenate([atm_mix, response], axis=0), high, high)
    )
    amat = jnp.concatenate([amix_hi, amix_lo, amix_hi], axis=1)
    coef = jnp.broadcast_to(
        (exchange_factor_array + LINK * exchange_response_matrix[:, air - 1])[:, None],
        (chan, cells_a),
    )
    dims = (rows, per_tile, chan, cells_a, cells_o, air - 1, (comp_count, lev_count))
    anywhere = pl.BlockSpec(memory_space=pl.ANY)
    vmem = pl.BlockSpec(memory_space=pltpu.VMEM)
    dma = pltpu.SemaphoreType.DMA
    ocean_end, atm_end, flux_end = pl.pallas_call(
        make_kernel(dims),
        out_shape=(
            jax.ShapeDtypeStruct((rows, deep, cells_o), F32),
            jax.ShapeDtypeStruct((rows, high, cells_a), F32),
            jax.ShapeDtypeStruct((rows, chan, cells_a), F32),
        ),
        in_specs=[anywhere, anywhere, vmem, anywhere] + [vmem] * 7,
        out_specs=(anywhere, anywhere, vmem),
        scratch_shapes=[
            pltpu.VMEM((rows, deep, cells_o), F32),
            pltpu.VMEM((rows, high, cells_a), F32),
            pltpu.VMEM((rows, per_tile * cells_a, cells_o), BF16),
            pltpu.VMEM((chan, pairs, cells_o), F32),
            pltpu.VMEM((9, chan, rows, cells_o), BF16),
            pltpu.VMEM((9, chan, rows, cells_o), BF16),
            pltpu.VMEM((9, rows, cells_o), BF16),
            pltpu.VMEM((rows, 16, cells_o), BF16),
            pltpu.VMEM((8, 128), F32),
            pltpu.VMEM((rows, 3 * deep + 4 * chan, cells_o), BF16),
            pltpu.VMEM((rows, 3 * high, cells_a), BF16),
            pltpu.VMEM((rows, 8, cells_a), F32),
            pltpu.VMEM((STEPS, 2, deep, cells_o), F32),
            pltpu.VMEM((STEPS, 2, deep, 128), F32),
            pltpu.VMEM((2, deep, 128), F32),
            pltpu.VMEM((STEPS, 2, high, cells_a), F32),
            pltpu.VMEM((STEPS, 2, high, 128), F32),
            pltpu.VMEM((2, high, 128), F32),
            dma((2,)),
            dma((rows,)),
            dma((9,)),
            dma((9,)),
            dma((9,)),
            dma((9,)),
            dma((STEPS, 4)),
            dma((STEPS, 4)),
            dma((STEPS, 4)),
            dma((STEPS, 4)),
        ],
        compiler_params=pltpu.CompilerParams(
            collective_id=0, has_side_effects=True, vmem_limit_bytes=40 * 1024 * 1024
        ),
        name="coupled",
    )(
        ocean_t, atm_t, flux_t,
        pair_weight.reshape(rows, per_tile * cells_a, cells_o),
        surface, slot.reshape(1, pairs), slot_col, omat, amat, coef, sea_mask.astype(F32),
    )
    return (
        atm_end[:, :air].transpose(1, 0, 2),
        ocean_end[:, :sea].transpose(1, 0, 2),
        (flux_end / STEPS).transpose(1, 0, 2).astype(BF16),
    )


def solution(mesh):
    in_specs = (
        P("member", "comp", "lev"),
        P("member", "comp", "lev"),
        P("member", "comp", "lev"),
        P(("comp", "lev")),
        P(("comp", "lev")),
        P(("comp", "lev"), None, None),
        P(),
        P(),
        P(),
        P(),
        P(),
        P("comp", "lev"),
    )
    out_specs = (P("member", "comp", "lev"), P("member", "comp", "lev"), P("member", "comp", "lev"))
    return jax.shard_map(body, mesh=mesh, in_specs=in_specs, out_specs=out_specs, check_vma=False)
```

```python
import jax
import jax.numpy as jnp
from jax import lax
from jax.experimental import pallas as pl
from jax.experimental.pallas import tpu as pltpu
from jax.sharding import PartitionSpec as P

STEPS = 4
RATE = 0.24
LINK = 0.5
BF16 = jnp.bfloat16
F32 = jnp.float32
MESH = pl.DeviceIdType.MESH
NEAR = [(n // 3 - 1, n % 3 - 1) for n in range(9)]
SIDES = [(-1, 0), (1, 0), (0, -1), (0, 1)]


def halves(x):
    hi = x.astype(BF16)
    return hi, (x - hi.astype(F32)).astype(BF16)


def reflect(index, count):
    return jnp.where(
        index < 0, -index, jnp.where(index > count - 1, 2 * (count - 1) - index, index)
    )


def make_kernel(dims):
    rows, per_tile, chan, cells_a, cells_o, last, sea_levels, counts = dims
    pairs = rows * per_tile

    def kernel(
        atm_in, ocean_in, flux_in, offset_in, tile_in, weight_in, air_mix, sea_mix, response,
        factor, profile, sea,
        atm_out, ocean_out, flux_out,
        ocean_load, atm_load, ocean, atm, wbuf, prod, part, precv, surf, gathered, flux_ref,
        pick_ref, wanted, omat, amat, coef, wet, ou, au, sst,
        orow, ocol, oedge, arow, acol, aedge,
        in_sem, ol_sem, al_sem, w_sem, surf_send, surf_recv, part_send, part_recv,
        o_send, o_recv, a_send, a_recv,
    ):
        ci = lax.axis_index("comp")
        li = lax.axis_index("lev")
        comp_count, lev_count = counts

        def there(di, dj):
            ok = None
            for delta, index, count in ((di, ci, comp_count), (dj, li, lev_count)):
                if delta == -1:
                    one = index > 0
                elif delta == 1:
                    one = index < count - 1
                else:
                    continue
                ok = one if ok is None else jnp.logical_and(ok, one)
            return ok

        def device(di, dj):
            return {
                "comp": jnp.clip(ci + di, 0, comp_count - 1),
                "lev": jnp.clip(li + dj, 0, lev_count - 1),
            }

        loads = [
            pltpu.make_async_copy(
                source.at[:, pl.ds(128 * h, 128)], target.at[h], sem.at[h]
            )
            for source, target, sem in (
                (ocean_in, ocean_load, ol_sem), (atm_in, atm_load, al_sem)
            )
            for h in range(target.shape[0])
        ]
        for load in loads:
            load.start()

        def load_weight(y):
            return pltpu.make_async_copy(weight_in.at[y], wbuf.at[y], w_sem.at[y])

        def start_weight(y, carry):
            load_weight(y).start()
            return carry

        lax.fori_loop(0, rows, start_weight, 0)

        for n, (di, dj) in enumerate(NEAR):
            if n != 4:
                @pl.when(jnp.logical_not(there(di, dj)))
                def _():
                    surf[n] = jnp.zeros(surf.shape[1:], BF16)
        for side, (di, dj) in enumerate(SIDES):
            @pl.when(jnp.logical_not(there(di, dj)))
            def _():
                for rbuf, cbuf in ((orow, ocol), (arow, acol)):
                    buf = rbuf if side < 2 else cbuf
                    for s in range(STEPS):
                        buf[s, side % 2] = jnp.zeros(buf.shape[2:], F32)

        barrier = pltpu.get_barrier_semaphore()
        for n, (di, dj) in enumerate(NEAR):
            if n != 4:
                @pl.when(there(di, dj))
                def _():
                    pl.semaphore_signal(
                        barrier, inc=1, device_id=device(di, dj), device_id_type=MESH
                    )
        tall = 1 + (ci > 0).astype(jnp.int32) + (ci < comp_count - 1).astype(jnp.int32)
        wide = 1 + (li > 0).astype(jnp.int32) + (li < lev_count - 1).astype(jnp.int32)

        def remote(src, dst, send, recv, di, dj):
            return pltpu.make_async_remote_copy(
                src_ref=src, dst_ref=dst, send_sem=send, recv_sem=recv,
                device_id=device(di, dj), device_id_type=MESH,
            )

        def surf_copy(n):
            return remote(
                surf.at[4], surf.at[8 - n], surf_send.at[n], surf_recv.at[n], *NEAR[n]
            )

        def part_copy(n):
            return remote(
                part.at[n], precv.at[n], part_send.at[n], part_recv.at[n], *NEAR[n]
            )

        def side_copy(state, rbuf, cbuf, edge, send, recv, s, side):
            if side < 2:
                src = state.at[0 if side == 0 else rows - 1]
                dst = rbuf.at[s, 1 - side]
            else:
                src = edge.at[side - 2]
                dst = cbuf.at[s, 3 - side]
            return remote(
                src, dst, send.at[s, side], recv.at[s, side], *SIDES[side]
            )

        ocean_parts = (ocean, orow, ocol, oedge, o_send, o_recv)
        atm_parts = (atm, arow, acol, aedge, a_send, a_recv)

        def start_sides(parts, s):
            for side, (di, dj) in enumerate(SIDES):
                @pl.when(there(di, dj))
                def _():
                    side_copy(*parts, s, side).start()

        def wait_sent(parts, s):
            for side, (di, dj) in enumerate(SIDES):
                @pl.when(there(di, dj))
                def _():
                    side_copy(*parts, s, side).wait_send()

        def wait_sides(parts, s):
            for side, (di, dj) in enumerate(SIDES):
                @pl.when(there(-di, -dj))
                def _():
                    side_copy(*parts, s, side).wait_recv()

        def pack(slabs, edge):
            depth = edge.shape[1]
            lane = lax.broadcasted_iota(jnp.int32, (depth, 128), 1)
            left = jnp.zeros((depth, 128), F32)
            right = jnp.zeros((depth, 128), F32)
            for r in range(rows):
                first, final = slabs(r)
                left = jnp.where(lane == r, pltpu.roll(first, r, 1) if r else first, left)
                right = jnp.where(lane == r, pltpu.roll(final, r + 1, 1), right)
            edge[0] = left
            edge[1] = right

        def ends(state):
            width = state.shape[2]
            return lambda r: (state[r, :, 0:128], state[r, :, width - 128:width])

        def turned(source, state, levels):
            depth, width = state.shape[1:]
            for r in range(rows):
                for col in range(0, width, 128):
                    state[r, 0:levels, col:col + 128] = source[
                        col // 128, pl.ds(r, levels, stride=rows), :
                    ]
                if depth > levels:
                    state[r, levels:depth] = jnp.zeros((depth - levels, width), F32)

        for load in loads[:ocean_load.shape[0]]:
            load.wait()
        turned(ocean_load, ocean, sea_levels)
        for h in range(ocean_load.shape[0]):
            surf[4, :, 128 * h:128 * (h + 1)] = ocean_load[h, 0:rows].astype(BF16)
        pack(ends(ocean), oedge)
        for load in loads[ocean_load.shape[0]:]:
            load.wait()
        turned(atm_load, atm, last + 1)
        pack(ends(atm), aedge)

        def one_hot(shape, test):
            first = lax.broadcasted_iota(jnp.int32, shape, 0)
            second = lax.broadcasted_iota(jnp.int32, shape, 1)
            return test(first, second).astype(F32).astype(BF16)

        def placed(matrix, width, places):
            total = None
            for term, offsets in zip(halves(matrix), places):
                def test(k, j):
                    hit = j == k + offsets[0]
                    for offset in offsets[1:]:
                        hit = jnp.logical_or(hit, j == k + offset)
                    return hit

                piece = jnp.dot(
                    term, one_hot((matrix.shape[1], width), test), preferred_element_type=F32
                )
                total = piece if total is None else total + piece
            return total

        deep, high = ocean.shape[1], atm.shape[1]
        wide_o, wide_a = omat.shape[1], amat.shape[1]
        square = jnp.concatenate(
            [
                placed(sea_mix[...], wide_o, ((0, 2 * deep), (deep,)))
                + placed(
                    profile[...], wide_o,
                    ((3 * deep, 3 * deep + 2 * chan), (3 * deep + chan,)),
                ),
                jnp.zeros((deep - sea_levels, wide_o), F32),
            ],
            axis=0,
        )
        omat[...] = square.astype(BF16)
        both = jnp.concatenate(
            [
                air_mix[...],
                jnp.dot(
                    response[...], air_mix[...], precision=lax.Precision.HIGHEST,
                    preferred_element_type=F32,
                ),
            ],
            axis=0,
        )
        amat[...] = placed(both, wide_a, ((0, 2 * high), (high,))).astype(BF16)
        field = lax.broadcasted_iota(jnp.int32, (chan, cells_a), 0)
        factors = LINK * jnp.broadcast_to(response[:, last:last + 1], (chan, cells_a))
        for c in range(chan):
            factors = factors + jnp.where(field == c, factor[c], 0.0)
        coef[...] = factors
        wet[...] = sea[...].astype(F32)

        spot = one_hot(
            (rows * chan * per_tile, chan * rows),
            lambda k, j: j == (k // per_tile) % chan * rows + k // (per_tile * chan),
        )
        flux_ref[...] = jnp.dot(
            spot, flux_in[...], preferred_element_type=F32
        ).astype(BF16).reshape(rows, chan * per_tile, cells_a)

        slots = 9 * rows
        offset = offset_in[...]
        step_row = (offset >= 3).astype(jnp.int32) + (offset >= 6).astype(jnp.int32)
        dest_row = reflect(ci + step_row - 1, comp_count)
        dest_col = reflect(li + (offset - 3 * step_row) - 1, lev_count)
        slot = ((dest_row - ci + 1) * 3 + (dest_col - li + 1)) * rows + tile_in[...]
        pick_ref[...] = (
            lax.broadcasted_iota(jnp.int32, (slots, pairs), 0) == slot
        ).astype(F32).astype(BF16)
        group = 16
        owner = one_hot(
            (rows * group, pairs),
            lambda k, q: jnp.logical_and(
                q == k // group * per_tile + k % group, k % group < per_tile
            ),
        )
        wanted[...] = lax.dot_general(
            owner, pick_ref[...], (((1,), (1,)), ((), ())), preferred_element_type=F32
        ).astype(BF16)

        pl.semaphore_wait(barrier, tall * wide - 1)

        for n, (di, dj) in enumerate(NEAR):
            if n != 4:
                @pl.when(there(di, dj))
                def _():
                    surf_copy(n).start()
        start_sides(atm_parts, 0)
        start_sides(ocean_parts, 0)

        which = lax.broadcasted_iota(jnp.int32, (chan * per_tile, cells_a), 0) % per_tile

        def multiply(y, carry):
            load_weight(y).wait()
            flux = flux_ref[y]
            left = jnp.concatenate(
                [jnp.where(which == p, flux, 0.0).astype(BF16) for p in range(per_tile)], axis=1
            )
            out = jnp.dot(left, wbuf[y], preferred_element_type=F32)
            at = pl.ds(pl.multiple_of(y * per_tile, per_tile), per_tile)
            for c in range(chan):
                prod[c, at, :] = out[c * per_tile:(c + 1) * per_tile]
            return carry

        lax.fori_loop(0, rows, multiply, 0)

        pick = jnp.concatenate([pick_ref[...], pick_ref[...]], axis=1)
        for c in range(chan):
            hi, lo = halves(prod[c])
            sums = jnp.dot(
                pick, jnp.concatenate([hi, lo], axis=0), preferred_element_type=F32
            ).astype(BF16)
            for n in range(9):
                part[n, c] = sums[n * rows:(n + 1) * rows]
        for n, (di, dj) in enumerate(NEAR):
            if n != 4:
                @pl.when(there(di, dj))
                def _():
                    part_copy(n).start()

        for n, (di, dj) in enumerate(NEAR):
            if n != 4:
                @pl.when(there(-di, -dj))
                def _():
                    surf_copy(n).wait_recv()
        found = jnp.dot(wanted[...], surf[...].reshape(slots, cells_o), preferred_element_type=F32)
        spare = lax.broadcasted_iota(jnp.int32, (rows * group, cells_o), 0) % group >= per_tile
        gathered[...] = jnp.where(spare, 1.0, found).astype(BF16).reshape(rows, group, cells_o)
        line = lax.broadcasted_iota(jnp.int32, (8, cells_a), 0)

        def regrid(y, carry):
            out = lax.dot_general(
                gathered[y], wbuf[y], (((1,), (1,)), ((), ())), preferred_element_type=F32
            )
            num = jnp.zeros((8, cells_a), F32)
            den = jnp.zeros((8, cells_a), F32)
            for p in range(per_tile):
                cols = slice(p * cells_a, (p + 1) * cells_a)
                num = num + jnp.where(line == p, out[0:8, cols], 0.0)
                den = den + out[8:16, cols]
            total = jnp.sum(num, axis=0, keepdims=True)
            sst[y] = jnp.broadcast_to(total, (8, cells_a)) / den
            return carry

        lax.fori_loop(0, rows, regrid, 0)
        flux_out[...] = jnp.zeros_like(flux_out)

        def stencil(parts, s, r):
            state, rbuf, cbuf = parts[0], parts[1], parts[2]
            depth, width = state.shape[1], state.shape[2]
            lane = lax.broadcasted_iota(jnp.int32, (depth, 128), 1)
            x = state[r]
            up = rbuf[s, 0] if r == 0 else state[r - 1]
            down = rbuf[s, 1] if r == rows - 1 else state[r + 1]
            west = pltpu.roll(x, 1, 1)
            east = pltpu.roll(x, width - 1, 1)
            from_west = cbuf[s, 0]
            if r:
                from_west = pltpu.roll(from_west, 128 - r, 1)
            from_east = pltpu.roll(cbuf[s, 1], 127 - r, 1)
            west_end = jnp.where(lane == 0, from_west, west[:, 0:128])
            east_end = jnp.where(lane == 127, from_east, east[:, width - 128:width])
            if width > 128:
                west_end = jnp.concatenate([west_end, west[:, 128:]], axis=1)
                east_end = jnp.concatenate([east[:, 0:width - 128], east_end], axis=1)
            return (1.0 - 4.0 * RATE) * x + RATE * ((up + down) + (west_end + east_end))

        def step(s, carry):
            wait_sides(atm_parts, s)
            for r in range(rows):
                hi, lo = halves(stencil(atm_parts, s, r))
                au[r] = jnp.concatenate([hi, hi, lo], axis=0)
            wait_sent(atm_parts, s)
            depth = atm.shape[1]
            level = lax.broadcasted_iota(jnp.int32, (depth, cells_a), 0)
            for r in range(rows):
                mixed = jnp.dot(amat[...], au[r], preferred_element_type=F32)
                gap = sst[r, 0:1] - mixed[last:last + 1]
                flux_out[r] += mixed[last + 1:last + 1 + chan] + coef[...] * gap
                atm[r] = mixed + jnp.where(level == last, LINK * gap, 0.0)

            @pl.when(s < STEPS - 1)
            def _():
                pack(ends(atm), aedge)
                start_sides(atm_parts, s + 1)

            @pl.when(s == 0)
            def _():
                total = part[4].astype(F32).reshape(chan * rows, cells_o)
                prod[0, 0:chan * rows] = total
                for n, (di, dj) in enumerate(NEAR):
                    if n != 4:
                        @pl.when(there(-di, -dj))
                        def _():
                            part_copy(n).wait_recv()
                            prod[0, 0:chan * rows] += precv[n].astype(F32).reshape(
                                chan * rows, cells_o
                            )
                size = 4 * chan
                to = lax.broadcasted_iota(jnp.int32, (rows * size, chan * rows), 0)
                source = lax.broadcasted_iota(jnp.int32, (rows * size, chan * rows), 1)
                place = to % size
                turn = (
                    jnp.logical_and(
                        source == (place % chan) * rows + to // size, place < 3 * chan
                    )
                ).astype(F32).astype(BF16)
                hi, lo = halves(prod[0, 0:chan * rows])
                laid = jnp.dot(
                    jnp.concatenate([turn, turn], axis=1),
                    jnp.concatenate([hi, lo], axis=0),
                    preferred_element_type=F32,
                )
                high = laid.astype(BF16).astype(F32)
                at = lax.broadcasted_iota(jnp.int32, laid.shape, 0) % size
                both = jnp.where(at < 2 * chan, high, laid - high).astype(BF16)
                both = both.reshape(rows, size, cells_o)
                mixing = 3 * ocean.shape[1]
                for r in range(rows):
                    ou[r, mixing:mixing + size] = both[r]

            wait_sides(ocean_parts, s)
            for r in range(rows):
                hi, lo = halves(stencil(ocean_parts, s, r))
                ou[r, 0:3 * deep] = jnp.concatenate([hi, hi, lo], axis=0)
            wait_sent(ocean_parts, s)
            for r in range(rows):
                ocean[r] = wet[r:r + 1] * jnp.dot(
                    omat[...], ou[r], preferred_element_type=F32
                )

            @pl.when(s < STEPS - 1)
            def _():
                pack(ends(ocean), oedge)
                start_sides(ocean_parts, s + 1)

            return carry

        lax.fori_loop(0, STEPS, step, 0)

        save_ocean = pltpu.make_async_copy(ocean, ocean_out, in_sem.at[0])
        save_atm = pltpu.make_async_copy(atm, atm_out, in_sem.at[1])
        save_ocean.start()
        save_atm.start()
        for n, (di, dj) in enumerate(NEAR):
            if n != 4:
                @pl.when(there(di, dj))
                def _():
                    surf_copy(n).wait_send()
                    part_copy(n).wait_send()
        save_ocean.wait()
        save_atm.wait()

    return kernel


def body(
    atm_state,
    ocean_state,
    flux_prev,
    pair_offset,
    pair_tile,
    pair_weight,
    atm_mix,
    ocean_mix,
    exchange_response_matrix,
    exchange_factor_array,
    depth_profile,
    sea_mask,
):
    comp_count = lax.axis_size("comp")
    lev_count = lax.axis_size("lev")
    pairs, cells_a, cells_o = pair_weight.shape
    air, rows = atm_state.shape[:2]
    sea = ocean_state.shape[0]
    chan = flux_prev.shape[0]
    per_tile = pairs // rows
    deep = (sea + 15) // 16 * 16
    high = (air + chan + 15) // 16 * 16
    dims = (rows, per_tile, chan, cells_a, cells_o, air - 1, sea, (comp_count, lev_count))
    anywhere = pl.BlockSpec(memory_space=pl.ANY)
    vmem = pl.BlockSpec(memory_space=pltpu.VMEM)
    dma = pltpu.SemaphoreType.DMA
    smem = pl.BlockSpec(memory_space=pltpu.SMEM)
    atm_end, ocean_end, flux_end = pl.pallas_call(
        make_kernel(dims),
        out_shape=(
            jax.ShapeDtypeStruct((rows, high, cells_a), F32),
            jax.ShapeDtypeStruct((rows, deep, cells_o), F32),
            jax.ShapeDtypeStruct((rows, chan, cells_a), F32),
        ),
        in_specs=[anywhere, anywhere, vmem, vmem, vmem, anywhere, vmem, vmem, vmem, smem, vmem, vmem],
        out_specs=(anywhere, anywhere, vmem),
        scratch_shapes=[
            pltpu.VMEM((cells_o // 128, sea * rows, 128), F32),
            pltpu.VMEM((cells_a // 128, air * rows, 128), F32),
            pltpu.VMEM((rows, deep, cells_o), F32),
            pltpu.VMEM((rows, high, cells_a), F32),
            pltpu.VMEM((rows, per_tile * cells_a, cells_o), BF16),
            pltpu.VMEM((chan, pairs, cells_o), F32),
            pltpu.VMEM((9, chan, rows, cells_o), BF16),
            pltpu.VMEM((9, chan, rows, cells_o), BF16),
            pltpu.VMEM((9, rows, cells_o), BF16),
            pltpu.VMEM((rows, 16, cells_o), BF16),
            pltpu.VMEM((rows, chan * per_tile, cells_a), BF16),
            pltpu.VMEM((9 * rows, pairs), BF16),
            pltpu.VMEM((rows * 16, 9 * rows), BF16),
            pltpu.VMEM((deep, 3 * deep + 4 * chan), BF16),
            pltpu.VMEM((high, 3 * high), BF16),
            pltpu.VMEM((chan, cells_a), F32),
            pltpu.VMEM((rows, cells_o), F32),
            pltpu.VMEM((rows, 3 * deep + 4 * chan, cells_o), BF16),
            pltpu.VMEM((rows, 3 * high, cells_a), BF16),
            pltpu.VMEM((rows, 8, cells_a), F32),
            pltpu.VMEM((STEPS, 2, deep, cells_o), F32),
            pltpu.VMEM((STEPS, 2, deep, 128), F32),
            pltpu.VMEM((2, deep, 128), F32),
            pltpu.VMEM((STEPS, 2, high, cells_a), F32),
            pltpu.VMEM((STEPS, 2, high, 128), F32),
            pltpu.VMEM((2, high, 128), F32),
            dma((2,)),
            dma((cells_o // 128,)),
            dma((cells_a // 128,)),
            dma((rows,)),
            dma((9,)),
            dma((9,)),
            dma((9,)),
            dma((9,)),
            dma((STEPS, 4)),
            dma((STEPS, 4)),
            dma((STEPS, 4)),
            dma((STEPS, 4)),
        ],
        compiler_params=pltpu.CompilerParams(
            collective_id=0, has_side_effects=True, vmem_limit_bytes=40 * 1024 * 1024
        ),
        name="coupled",
    )(
        atm_state.reshape(air * rows, cells_a),
        ocean_state.reshape(sea * rows, cells_o),
        flux_prev.reshape(chan * rows, cells_a),
        pair_offset.reshape(1, pairs),
        pair_tile.reshape(1, pairs),
        pair_weight.reshape(rows, per_tile * cells_a, cells_o),
        atm_mix, ocean_mix, exchange_response_matrix, exchange_factor_array, depth_profile, sea_mask,
    )
    return (
        atm_end[:, :air].transpose(1, 0, 2),
        ocean_end[:, :sea].transpose(1, 0, 2),
        (flux_end / STEPS).transpose(1, 0, 2).astype(BF16),
    )


def solution(mesh):
    in_specs = (
        P("member", "comp", "lev"),
        P("member", "comp", "lev"),
        P("member", "comp", "lev"),
        P(("comp", "lev")),
        P(("comp", "lev")),
        P(("comp", "lev"), None, None),
        P(),
        P(),
        P(),
        P(),
        P(),
        P("comp", "lev"),
    )
    out_specs = (P("member", "comp", "lev"), P("member", "comp", "lev"), P("member", "comp", "lev"))
    return jax.shard_map(body, mesh=mesh, in_specs=in_specs, out_specs=out_specs, check_vma=False)
```

```python
import jax
import jax.numpy as jnp
from jax import lax
from jax.experimental import pallas as pl
from jax.experimental.pallas import tpu as pltpu
from jax.sharding import PartitionSpec as P

STEPS = 4
RATE = 0.24
LINK = 0.5
BF16 = jnp.bfloat16
F32 = jnp.float32
MESH = pl.DeviceIdType.MESH
NEAR = [(n // 3 - 1, n % 3 - 1) for n in range(9)]
SIDES = [(-1, 0), (1, 0), (0, -1), (0, 1)]


def halves(x):
    hi = x.astype(BF16)
    return hi, (x - hi.astype(F32)).astype(BF16)


def reflect(index, count):
    return jnp.where(
        index < 0, -index, jnp.where(index > count - 1, 2 * (count - 1) - index, index)
    )


def make_kernel(dims):
    rows, per_tile, chan, cells_a, cells_o, last, sea_levels, counts = dims
    pairs = rows * per_tile

    def kernel(
        atm_in, ocean_in, flux_far, offset_far, tile_far, weight_in, air_far, sea_far,
        response_far, factor_far, profile_far, mask_far,
        atm_out, ocean_out, flux_out,
        flux_in, offset_in, tile_in, air_mix, sea_mix, response, factor, profile, sea,
        ocean_load, atm_load, ocean, atm, wbuf, prod, part, precv, surf, gathered, flux_ref,
        pick_ref, wanted, omat, amat, coef, wet, ou, au, sst,
        orow, ocol, oedge, arow, acol, aedge,
        in_sem, small_sem, ol_sem, al_sem, w_sem, surf_send, surf_recv, part_send, part_recv,
        o_send, o_recv, a_send, a_recv,
    ):
        ci = lax.axis_index("comp")
        li = lax.axis_index("lev")
        comp_count, lev_count = counts

        def there(di, dj):
            ok = None
            for delta, index, count in ((di, ci, comp_count), (dj, li, lev_count)):
                if delta == -1:
                    one = index > 0
                elif delta == 1:
                    one = index < count - 1
                else:
                    continue
                ok = one if ok is None else jnp.logical_and(ok, one)
            return ok

        def device(di, dj):
            return {
                "comp": jnp.clip(ci + di, 0, comp_count - 1),
                "lev": jnp.clip(li + dj, 0, lev_count - 1),
            }

        loads = [
            pltpu.make_async_copy(
                source.at[:, pl.ds(128 * h, 128)], target.at[h], sem.at[h]
            )
            for source, target, sem in (
                (ocean_in, ocean_load, ol_sem), (atm_in, atm_load, al_sem)
            )
            for h in range(target.shape[0])
        ]
        for load in loads:
            load.start()
        small = [
            pltpu.make_async_copy(source, target, small_sem.at[k])
            for k, (source, target) in enumerate((
                (flux_far, flux_in), (offset_far, offset_in), (tile_far, tile_in),
                (air_far, air_mix), (sea_far, sea_mix), (response_far, response),
                (factor_far, factor), (profile_far, profile), (mask_far, sea),
            ))
        ]
        for load in small:
            load.start()

        def load_weight(y):
            return pltpu.make_async_copy(weight_in.at[y], wbuf.at[y], w_sem.at[y])

        def start_weight(y, carry):
            load_weight(y).start()
            return carry

        lax.fori_loop(0, rows, start_weight, 0)

        for n, (di, dj) in enumerate(NEAR):
            if n != 4:
                @pl.when(jnp.logical_not(there(di, dj)))
                def _():
                    surf[n] = jnp.zeros(surf.shape[1:], BF16)
        for side, (di, dj) in enumerate(SIDES):
            @pl.when(jnp.logical_not(there(di, dj)))
            def _():
                for rbuf, cbuf in ((orow, ocol), (arow, acol)):
                    buf = rbuf if side < 2 else cbuf
                    for s in range(STEPS):
                        buf[s, side % 2] = jnp.zeros(buf.shape[2:], F32)

        barrier = pltpu.get_barrier_semaphore()
        for n, (di, dj) in enumerate(NEAR):
            if n != 4:
                @pl.when(there(di, dj))
                def _():
                    pl.semaphore_signal(
                        barrier, inc=1, device_id=device(di, dj), device_id_type=MESH
                    )
        tall = 1 + (ci > 0).astype(jnp.int32) + (ci < comp_count - 1).astype(jnp.int32)
        wide = 1 + (li > 0).astype(jnp.int32) + (li < lev_count - 1).astype(jnp.int32)

        def remote(src, dst, send, recv, di, dj):
            return pltpu.make_async_remote_copy(
                src_ref=src, dst_ref=dst, send_sem=send, recv_sem=recv,
                device_id=device(di, dj), device_id_type=MESH,
            )

        def surf_copy(n):
            return remote(
                surf.at[4], surf.at[8 - n], surf_send.at[n], surf_recv.at[n], *NEAR[n]
            )

        def part_copy(n):
            return remote(
                part.at[n], precv.at[n], part_send.at[n], part_recv.at[n], *NEAR[n]
            )

        def side_copy(state, rbuf, cbuf, edge, send, recv, s, side):
            if side < 2:
                src = state.at[0 if side == 0 else rows - 1]
                dst = rbuf.at[s, 1 - side]
            else:
                src = edge.at[side - 2]
                dst = cbuf.at[s, 3 - side]
            return remote(
                src, dst, send.at[s, side], recv.at[s, side], *SIDES[side]
            )

        ocean_parts = (ocean, orow, ocol, oedge, o_send, o_recv)
        atm_parts = (atm, arow, acol, aedge, a_send, a_recv)

        def start_sides(parts, s, sides=(0, 1, 2, 3)):
            for side in sides:
                di, dj = SIDES[side]

                @pl.when(there(di, dj))
                def _():
                    side_copy(*parts, s, side).start()

        def wait_sent(parts, s):
            for side, (di, dj) in enumerate(SIDES):
                @pl.when(there(di, dj))
                def _():
                    side_copy(*parts, s, side).wait_send()

        def wait_sides(parts, s, sides):
            for side in sides:
                di, dj = SIDES[side]

                @pl.when(there(-di, -dj))
                def _():
                    side_copy(*parts, s, side).wait_recv()

        def pack(slabs, edge):
            depth = edge.shape[1]
            lane = lax.broadcasted_iota(jnp.int32, (depth, 128), 1)
            left = jnp.zeros((depth, 128), F32)
            right = jnp.zeros((depth, 128), F32)
            for r in range(rows):
                first, final = slabs(r)
                left = jnp.where(lane == r, pltpu.roll(first, r, 1) if r else first, left)
                right = jnp.where(lane == r, pltpu.roll(final, r + 1, 1), right)
            edge[0] = left
            edge[1] = right

        def ends(state):
            width = state.shape[2]
            return lambda r: (state[r, :, 0:128], state[r, :, width - 128:width])

        def turned(source, state, levels):
            depth, width = state.shape[1:]
            for r in range(rows):
                for col in range(0, width, 128):
                    state[r, 0:levels, col:col + 128] = source[
                        col // 128, pl.ds(r, levels, stride=rows), :
                    ]
                if depth > levels:
                    state[r, levels:depth] = jnp.zeros((depth - levels, width), F32)

        for load in loads[:ocean_load.shape[0]]:
            load.wait()
        turned(ocean_load, ocean, sea_levels)
        for h in range(ocean_load.shape[0]):
            surf[4, :, 128 * h:128 * (h + 1)] = ocean_load[h, 0:rows].astype(BF16)
        pack(ends(ocean), oedge)
        for load in loads[ocean_load.shape[0]:]:
            load.wait()
        turned(atm_load, atm, last + 1)
        pack(ends(atm), aedge)

        for load in small:
            load.wait()

        def one_hot(shape, test):
            first = lax.broadcasted_iota(jnp.int32, shape, 0)
            second = lax.broadcasted_iota(jnp.int32, shape, 1)
            return test(first, second).astype(F32).astype(BF16)

        def placed(matrix, width, places, inner=1):
            total = None
            for term, offsets in zip(halves(matrix), places):
                def test(k, j):
                    hit = j == k + offsets[0]
                    for offset in offsets[1:]:
                        hit = jnp.logical_or(hit, j == k + offset)
                    return hit

                piece = lax.dot_general(
                    term, one_hot((matrix.shape[inner], width), test),
                    (((inner,), (0,)), ((), ())), preferred_element_type=F32,
                )
                total = piece if total is None else total + piece
            return total

        deep, high = ocean.shape[1], atm.shape[1]
        wide_o, wide_a = omat.shape[1], amat.shape[1]
        square = jnp.concatenate(
            [
                placed(sea_mix[...], wide_o, ((0, 2 * deep), (deep,)))
                + placed(
                    profile[...], wide_o,
                    ((3 * deep, 3 * deep + 2 * chan), (3 * deep + chan,)), 0,
                ),
                jnp.zeros((deep - sea_levels, wide_o), F32),
            ],
            axis=0,
        )
        omat[...] = square.astype(BF16)
        both = jnp.concatenate(
            [
                air_mix[...],
                jnp.dot(
                    response[...], air_mix[...], precision=lax.Precision.HIGHEST,
                    preferred_element_type=F32,
                ),
            ],
            axis=0,
        )
        amat[...] = placed(both, wide_a, ((0, 2 * high), (high,))).astype(BF16)
        field = lax.broadcasted_iota(jnp.int32, (chan, cells_a), 0)
        factors = LINK * jnp.broadcast_to(response[:, last:last + 1], (chan, cells_a))
        for c in range(chan):
            factors = factors + jnp.where(field == c, factor[c], 0.0)
        coef[...] = factors
        wet[...] = sea[...].astype(F32)

        spot = one_hot(
            (rows * chan * per_tile, chan * rows),
            lambda k, j: j == (k // per_tile) % chan * rows + k // (per_tile * chan),
        )
        flux_ref[...] = jnp.dot(
            spot, flux_in[...], preferred_element_type=F32
        ).astype(BF16).reshape(rows, chan * per_tile, cells_a)

        slots = 9 * rows
        offset = offset_in[...]
        step_row = (offset >= 3).astype(jnp.int32) + (offset >= 6).astype(jnp.int32)
        dest_row = reflect(ci + step_row - 1, comp_count)
        dest_col = reflect(li + (offset - 3 * step_row) - 1, lev_count)
        slot = ((dest_row - ci + 1) * 3 + (dest_col - li + 1)) * rows + tile_in[...]
        pick_ref[...] = (
            lax.broadcasted_iota(jnp.int32, (slots, pairs), 0) == slot
        ).astype(F32).astype(BF16)
        group = 16
        owner = one_hot(
            (rows * group, pairs),
            lambda k, q: jnp.logical_and(
                q == k // group * per_tile + k % group, k % group < per_tile
            ),
        )
        wanted[...] = lax.dot_general(
            owner, pick_ref[...], (((1,), (1,)), ((), ())), preferred_element_type=F32
        ).astype(BF16)

        pl.semaphore_wait(barrier, tall * wide - 1)

        for n, (di, dj) in enumerate(NEAR):
            if n != 4:
                @pl.when(there(di, dj))
                def _():
                    surf_copy(n).start()
        start_sides(atm_parts, 0)
        start_sides(ocean_parts, 0)

        which = lax.broadcasted_iota(jnp.int32, (chan * per_tile, cells_a), 0) % per_tile

        def multiply(y, carry):
            load_weight(y).wait()
            flux = flux_ref[y]
            left = jnp.concatenate(
                [jnp.where(which == p, flux, 0.0).astype(BF16) for p in range(per_tile)], axis=1
            )
            out = jnp.dot(left, wbuf[y], preferred_element_type=F32)
            at = pl.ds(pl.multiple_of(y * per_tile, per_tile), per_tile)
            for c in range(chan):
                prod[c, at, :] = out[c * per_tile:(c + 1) * per_tile]
            return carry

        lax.fori_loop(0, rows, multiply, 0)

        pick = jnp.concatenate([pick_ref[...], pick_ref[...]], axis=1)
        for c in range(chan):
            hi, lo = halves(prod[c])
            sums = jnp.dot(
                pick, jnp.concatenate([hi, lo], axis=0), preferred_element_type=F32
            ).astype(BF16)
            for n in range(9):
                part[n, c] = sums[n * rows:(n + 1) * rows]
        for n, (di, dj) in enumerate(NEAR):
            if n != 4:
                @pl.when(there(di, dj))
                def _():
                    part_copy(n).start()

        for n, (di, dj) in enumerate(NEAR):
            if n != 4:
                @pl.when(there(-di, -dj))
                def _():
                    surf_copy(n).wait_recv()
        found = jnp.dot(wanted[...], surf[...].reshape(slots, cells_o), preferred_element_type=F32)
        spare = lax.broadcasted_iota(jnp.int32, (rows * group, cells_o), 0) % group >= per_tile
        gathered[...] = jnp.where(spare, 1.0, found).astype(BF16).reshape(rows, group, cells_o)
        line = lax.broadcasted_iota(jnp.int32, (8, cells_a), 0)

        def regrid(y, carry):
            out = lax.dot_general(
                gathered[y], wbuf[y], (((1,), (1,)), ((), ())), preferred_element_type=F32
            )
            num = jnp.zeros((8, cells_a), F32)
            den = jnp.zeros((8, cells_a), F32)
            for p in range(per_tile):
                cols = slice(p * cells_a, (p + 1) * cells_a)
                num = num + jnp.where(line == p, out[0:8, cols], 0.0)
                den = den + out[8:16, cols]
            total = jnp.sum(num, axis=0, keepdims=True)
            sst[y] = jnp.broadcast_to(total, (8, cells_a)) / den
            return carry

        lax.fori_loop(0, rows, regrid, 0)
        flux_out[...] = jnp.zeros_like(flux_out)

        def stencil(parts, s, r):
            state, rbuf, cbuf = parts[0], parts[1], parts[2]
            depth, width = state.shape[1], state.shape[2]
            lane = lax.broadcasted_iota(jnp.int32, (depth, 128), 1)
            x = state[r]
            up = rbuf[s, 0] if r == 0 else state[r - 1]
            down = rbuf[s, 1] if r == rows - 1 else state[r + 1]
            west = pltpu.roll(x, 1, 1)
            east = pltpu.roll(x, width - 1, 1)
            from_west = cbuf[s, 0]
            if r:
                from_west = pltpu.roll(from_west, 128 - r, 1)
            from_east = pltpu.roll(cbuf[s, 1], 127 - r, 1)
            west_end = jnp.where(lane == 0, from_west, west[:, 0:128])
            east_end = jnp.where(lane == 127, from_east, east[:, width - 128:width])
            if width > 128:
                west_end = jnp.concatenate([west_end, west[:, 128:]], axis=1)
                east_end = jnp.concatenate([east[:, 0:width - 128], east_end], axis=1)
            return (1.0 - 4.0 * RATE) * x + RATE * ((up + down) + (west_end + east_end))

        def step(s, carry):
            def spread_atm(r):
                hi, lo = halves(stencil(atm_parts, s, r))
                au[r] = jnp.concatenate([hi, hi, lo], axis=0)

            wait_sides(atm_parts, s, (2, 3))
            for r in range(1, rows - 1):
                spread_atm(r)
            wait_sides(atm_parts, s, (0, 1))
            spread_atm(0)
            spread_atm(rows - 1)
            wait_sent(atm_parts, s)
            depth = atm.shape[1]
            level = lax.broadcasted_iota(jnp.int32, (depth, cells_a), 0)
            def mix_atm(r):
                mixed = jnp.dot(amat[...], au[r], preferred_element_type=F32)
                gap = sst[r, 0:1] - mixed[last:last + 1]
                flux_out[r] += mixed[last + 1:last + 1 + chan] + coef[...] * gap
                atm[r] = mixed + jnp.where(level == last, LINK * gap, 0.0)

            mix_atm(0)
            mix_atm(rows - 1)

            @pl.when(s < STEPS - 1)
            def _():
                start_sides(atm_parts, s + 1, (0, 1))

            for r in range(1, rows - 1):
                mix_atm(r)

            @pl.when(s < STEPS - 1)
            def _():
                pack(ends(atm), aedge)
                start_sides(atm_parts, s + 1, (2, 3))

            @pl.when(s == 0)
            def _():
                total = part[4].astype(F32).reshape(chan * rows, cells_o)
                prod[0, 0:chan * rows] = total
                for n, (di, dj) in enumerate(NEAR):
                    if n != 4:
                        @pl.when(there(-di, -dj))
                        def _():
                            part_copy(n).wait_recv()
                            prod[0, 0:chan * rows] += precv[n].astype(F32).reshape(
                                chan * rows, cells_o
                            )
                size = 4 * chan
                to = lax.broadcasted_iota(jnp.int32, (rows * size, chan * rows), 0)
                source = lax.broadcasted_iota(jnp.int32, (rows * size, chan * rows), 1)
                place = to % size
                turn = (
                    jnp.logical_and(
                        source == (place % chan) * rows + to // size, place < 3 * chan
                    )
                ).astype(F32).astype(BF16)
                hi, lo = halves(prod[0, 0:chan * rows])
                laid = jnp.dot(
                    jnp.concatenate([turn, turn], axis=1),
                    jnp.concatenate([hi, lo], axis=0),
                    preferred_element_type=F32,
                )
                high = laid.astype(BF16).astype(F32)
                at = lax.broadcasted_iota(jnp.int32, laid.shape, 0) % size
                both = jnp.where(at < 2 * chan, high, laid - high).astype(BF16)
                both = both.reshape(rows, size, cells_o)
                mixing = 3 * ocean.shape[1]
                for r in range(rows):
                    ou[r, mixing:mixing + size] = both[r]

            def spread_ocean(r):
                hi, lo = halves(stencil(ocean_parts, s, r))
                ou[r, 0:3 * deep] = jnp.concatenate([hi, hi, lo], axis=0)

            def mix_ocean(r):
                ocean[r] = wet[r:r + 1] * jnp.dot(
                    omat[...], ou[r], preferred_element_type=F32
                )

            wait_sides(ocean_parts, s, (2, 3))
            for r in range(1, rows - 1):
                spread_ocean(r)
            wait_sides(ocean_parts, s, (0, 1))
            spread_ocean(0)
            spread_ocean(rows - 1)
            wait_sent(ocean_parts, s)
            mix_ocean(0)
            mix_ocean(rows - 1)

            @pl.when(s < STEPS - 1)
            def _():
                start_sides(ocean_parts, s + 1, (0, 1))

            for r in range(1, rows - 1):
                mix_ocean(r)

            @pl.when(s < STEPS - 1)
            def _():
                pack(ends(ocean), oedge)
                start_sides(ocean_parts, s + 1, (2, 3))

            return carry

        lax.fori_loop(0, STEPS, step, 0)

        save_ocean = pltpu.make_async_copy(ocean, ocean_out, in_sem.at[0])
        save_atm = pltpu.make_async_copy(atm, atm_out, in_sem.at[1])
        save_ocean.start()
        save_atm.start()
        for n, (di, dj) in enumerate(NEAR):
            if n != 4:
                @pl.when(there(di, dj))
                def _():
                    surf_copy(n).wait_send()
                    part_copy(n).wait_send()
        save_ocean.wait()
        save_atm.wait()

    return kernel


def body(
    atm_state,
    ocean_state,
    flux_prev,
    pair_offset,
    pair_tile,
    pair_weight,
    atm_mix,
    ocean_mix,
    exchange_response_matrix,
    exchange_factor_array,
    depth_profile,
    sea_mask,
):
    comp_count = lax.axis_size("comp")
    lev_count = lax.axis_size("lev")
    pairs, cells_a, cells_o = pair_weight.shape
    air, rows = atm_state.shape[:2]
    sea = ocean_state.shape[0]
    chan = flux_prev.shape[0]
    per_tile = pairs // rows
    deep = (sea + 15) // 16 * 16
    high = (air + chan + 15) // 16 * 16
    dims = (rows, per_tile, chan, cells_a, cells_o, air - 1, sea, (comp_count, lev_count))
    anywhere = pl.BlockSpec(memory_space=pl.ANY)
    vmem = pl.BlockSpec(memory_space=pltpu.VMEM)
    dma = pltpu.SemaphoreType.DMA
    atm_end, ocean_end, flux_end = pl.pallas_call(
        make_kernel(dims),
        out_shape=(
            jax.ShapeDtypeStruct((rows, high, cells_a), F32),
            jax.ShapeDtypeStruct((rows, deep, cells_o), F32),
            jax.ShapeDtypeStruct((rows, chan, cells_a), F32),
        ),
        in_specs=[anywhere] * 12,
        out_specs=(anywhere, anywhere, vmem),
        scratch_shapes=[
            pltpu.VMEM((chan * rows, cells_a), BF16),
            pltpu.VMEM((1, pairs), jnp.int32),
            pltpu.VMEM((1, pairs), jnp.int32),
            pltpu.VMEM((air, air), F32),
            pltpu.VMEM((sea, sea), F32),
            pltpu.VMEM((chan, air), F32),
            pltpu.SMEM((chan,), F32),
            pltpu.VMEM((chan, sea), F32),
            pltpu.VMEM((rows, cells_o), jnp.int32),
            pltpu.VMEM((cells_o // 128, sea * rows, 128), F32),
            pltpu.VMEM((cells_a // 128, air * rows, 128), F32),
            pltpu.VMEM((rows, deep, cells_o), F32),
            pltpu.VMEM((rows, high, cells_a), F32),
            pltpu.VMEM((rows, per_tile * cells_a, cells_o), BF16),
            pltpu.VMEM((chan, pairs, cells_o), F32),
            pltpu.VMEM((9, chan, rows, cells_o), BF16),
            pltpu.VMEM((9, chan, rows, cells_o), BF16),
            pltpu.VMEM((9, rows, cells_o), BF16),
            pltpu.VMEM((rows, 16, cells_o), BF16),
            pltpu.VMEM((rows, chan * per_tile, cells_a), BF16),
            pltpu.VMEM((9 * rows, pairs), BF16),
            pltpu.VMEM((rows * 16, 9 * rows), BF16),
            pltpu.VMEM((deep, 3 * deep + 4 * chan), BF16),
            pltpu.VMEM((high, 3 * high), BF16),
            pltpu.VMEM((chan, cells_a), F32),
            pltpu.VMEM((rows, cells_o), F32),
            pltpu.VMEM((rows, 3 * deep + 4 * chan, cells_o), BF16),
            pltpu.VMEM((rows, 3 * high, cells_a), BF16),
            pltpu.VMEM((rows, 8, cells_a), F32),
            pltpu.VMEM((STEPS, 2, deep, cells_o), F32),
            pltpu.VMEM((STEPS, 2, deep, 128), F32),
            pltpu.VMEM((2, deep, 128), F32),
            pltpu.VMEM((STEPS, 2, high, cells_a), F32),
            pltpu.VMEM((STEPS, 2, high, 128), F32),
            pltpu.VMEM((2, high, 128), F32),
            dma((2,)),
            dma((9,)),
            dma((cells_o // 128,)),
            dma((cells_a // 128,)),
            dma((rows,)),
            dma((9,)),
            dma((9,)),
            dma((9,)),
            dma((9,)),
            dma((STEPS, 4)),
            dma((STEPS, 4)),
            dma((STEPS, 4)),
            dma((STEPS, 4)),
        ],
        compiler_params=pltpu.CompilerParams(
            collective_id=0, has_side_effects=True, vmem_limit_bytes=60 * 1024 * 1024
        ),
        name="coupled",
    )(
        atm_state.reshape(air * rows, cells_a),
        ocean_state.reshape(sea * rows, cells_o),
        flux_prev.reshape(chan * rows, cells_a),
        pair_offset.reshape(1, pairs),
        pair_tile.reshape(1, pairs),
        pair_weight.reshape(rows, per_tile * cells_a, cells_o),
        atm_mix, ocean_mix, exchange_response_matrix, exchange_factor_array,
        depth_profile.T, sea_mask,
    )
    return (
        atm_end[:, :air].transpose(1, 0, 2),
        ocean_end[:, :sea].transpose(1, 0, 2),
        (flux_end / STEPS).transpose(1, 0, 2).astype(BF16),
    )


def solution(mesh):
    in_specs = (
        P("member", "comp", "lev"),
        P("member", "comp", "lev"),
        P("member", "comp", "lev"),
        P(("comp", "lev")),
        P(("comp", "lev")),
        P(("comp", "lev"), None, None),
        P(),
        P(),
        P(),
        P(),
        P(),
        P("comp", "lev"),
    )
    out_specs = (P("member", "comp", "lev"), P("member", "comp", "lev"), P("member", "comp", "lev"))
    return jax.shard_map(body, mesh=mesh, in_specs=in_specs, out_specs=out_specs, check_vma=False)
```

```python
import jax
import jax.numpy as jnp
from jax import lax
from jax.experimental import pallas as pl
from jax.experimental.pallas import tpu as pltpu
from jax.sharding import PartitionSpec as P

STEPS = 4
RATE = 0.24
LINK = 0.5
BF16 = jnp.bfloat16
F32 = jnp.float32
MESH = pl.DeviceIdType.MESH
NEAR = [(n // 3 - 1, n % 3 - 1) for n in range(9)]
SIDES = [(-1, 0), (1, 0), (0, -1), (0, 1)]


def halves(x):
    hi = x.astype(BF16)
    return hi, (x - hi.astype(F32)).astype(BF16)


def reflect(index, count):
    return jnp.where(
        index < 0, -index, jnp.where(index > count - 1, 2 * (count - 1) - index, index)
    )


def make_kernel(dims):
    rows, per_tile, chan, cells_a, cells_o, last, sea_levels, counts = dims
    pairs = rows * per_tile

    def kernel(
        atm_in, ocean_in, flux_far, offset_far, tile_far, weight_in, air_far, sea_far,
        response_far, factor_far, profile_far, mask_far,
        atm_out, ocean_out, flux_far_out,
        flux_out, flux_sum, flux_end, flux_in, offset_in, tile_in, air_mix, sea_mix, response, factor, profile, sea,
        ocean_load, atm_load, ocean, atm, wbuf, prod, part, precv, surf, gathered, flux_ref,
        pick_ref, wanted, omat, amat, coef, wet, ou, au, sst,
        orow, ocol, oedge, arow, acol, aedge,
        in_sem, small_sem, ol_sem, al_sem, w_sem, surf_send, surf_recv, part_send, part_recv,
        o_send, o_recv, a_send, a_recv,
    ):
        ci = lax.axis_index("comp")
        li = lax.axis_index("lev")
        comp_count, lev_count = counts

        def there(di, dj):
            ok = None
            for delta, index, count in ((di, ci, comp_count), (dj, li, lev_count)):
                if delta == -1:
                    one = index > 0
                elif delta == 1:
                    one = index < count - 1
                else:
                    continue
                ok = one if ok is None else jnp.logical_and(ok, one)
            return ok

        def device(di, dj):
            return {
                "comp": jnp.clip(ci + di, 0, comp_count - 1),
                "lev": jnp.clip(li + dj, 0, lev_count - 1),
            }

        loads = [
            pltpu.make_async_copy(
                source.at[:, pl.ds(128 * h, 128)], target.at[h], sem.at[h]
            )
            for source, target, sem in (
                (ocean_in, ocean_load, ol_sem), (atm_in, atm_load, al_sem)
            )
            for h in range(target.shape[0])
        ]
        for load in loads:
            load.start()
        small = [
            pltpu.make_async_copy(source, target, small_sem.at[k])
            for k, (source, target) in enumerate((
                (flux_far, flux_in), (offset_far, offset_in), (tile_far, tile_in),
                (air_far, air_mix), (sea_far, sea_mix), (response_far, response),
                (factor_far, factor), (profile_far, profile), (mask_far, sea),
            ))
        ]
        for load in small:
            load.start()

        def load_weight(y):
            return pltpu.make_async_copy(weight_in.at[y], wbuf.at[y], w_sem.at[y])

        def start_weight(y, carry):
            load_weight(y).start()
            return carry

        lax.fori_loop(0, rows, start_weight, 0)

        for n, (di, dj) in enumerate(NEAR):
            if n != 4:
                @pl.when(jnp.logical_not(there(di, dj)))
                def _():
                    surf[n] = jnp.zeros(surf.shape[1:], BF16)
        for side, (di, dj) in enumerate(SIDES):
            @pl.when(jnp.logical_not(there(di, dj)))
            def _():
                for rbuf, cbuf in ((orow, ocol), (arow, acol)):
                    buf = rbuf if side < 2 else cbuf
                    for s in range(STEPS):
                        buf[s, side % 2] = jnp.zeros(buf.shape[2:], F32)

        barrier = pltpu.get_barrier_semaphore()
        for n, (di, dj) in enumerate(NEAR):
            if n != 4:
                @pl.when(there(di, dj))
                def _():
                    pl.semaphore_signal(
                        barrier, inc=1, device_id=device(di, dj), device_id_type=MESH
                    )
        tall = 1 + (ci > 0).astype(jnp.int32) + (ci < comp_count - 1).astype(jnp.int32)
        wide = 1 + (li > 0).astype(jnp.int32) + (li < lev_count - 1).astype(jnp.int32)

        def remote(src, dst, send, recv, di, dj):
            return pltpu.make_async_remote_copy(
                src_ref=src, dst_ref=dst, send_sem=send, recv_sem=recv,
                device_id=device(di, dj), device_id_type=MESH,
            )

        def surf_copy(n):
            return remote(
                surf.at[4], surf.at[8 - n], surf_send.at[n], surf_recv.at[n], *NEAR[n]
            )

        def part_copy(n):
            return remote(
                part.at[n], precv.at[n], part_send.at[n], part_recv.at[n], *NEAR[n]
            )

        def side_copy(state, rbuf, cbuf, edge, send, recv, s, side):
            if side < 2:
                src = state.at[0 if side == 0 else rows - 1]
                dst = rbuf.at[s, 1 - side]
            else:
                src = edge.at[side - 2]
                dst = cbuf.at[s, 3 - side]
            return remote(
                src, dst, send.at[s, side], recv.at[s, side], *SIDES[side]
            )

        ocean_parts = (ocean, orow, ocol, oedge, o_send, o_recv)
        atm_parts = (atm, arow, acol, aedge, a_send, a_recv)

        def start_sides(parts, s, sides=(0, 1, 2, 3)):
            for side in sides:
                di, dj = SIDES[side]

                @pl.when(there(di, dj))
                def _():
                    side_copy(*parts, s, side).start()

        def wait_sent(parts, s):
            for side, (di, dj) in enumerate(SIDES):
                @pl.when(there(di, dj))
                def _():
                    side_copy(*parts, s, side).wait_send()

        def wait_sides(parts, s, sides):
            for side in sides:
                di, dj = SIDES[side]

                @pl.when(there(-di, -dj))
                def _():
                    side_copy(*parts, s, side).wait_recv()

        def pack(slabs, edge):
            depth = edge.shape[1]
            lane = lax.broadcasted_iota(jnp.int32, (depth, 128), 1)
            left = jnp.zeros((depth, 128), F32)
            right = jnp.zeros((depth, 128), F32)
            for r in range(rows):
                first, final = slabs(r)
                left = jnp.where(lane == r, pltpu.roll(first, r, 1) if r else first, left)
                right = jnp.where(lane == r, pltpu.roll(final, r + 1, 1), right)
            edge[0] = left
            edge[1] = right

        def ends(state):
            width = state.shape[2]
            return lambda r: (state[r, :, 0:128], state[r, :, width - 128:width])

        def turned(source, state, levels):
            depth, width = state.shape[1:]
            for r in range(rows):
                for col in range(0, width, 128):
                    state[r, 0:levels, col:col + 128] = source[
                        col // 128, pl.ds(r, levels, stride=rows), :
                    ]
                if depth > levels:
                    state[r, levels:depth] = jnp.zeros((depth - levels, width), F32)

        for load in loads[:ocean_load.shape[0]]:
            load.wait()
        turned(ocean_load, ocean, sea_levels)
        for h in range(ocean_load.shape[0]):
            surf[4, :, 128 * h:128 * (h + 1)] = ocean_load[h, 0:rows].astype(BF16)
        pack(ends(ocean), oedge)
        for load in loads[ocean_load.shape[0]:]:
            load.wait()
        turned(atm_load, atm, last + 1)
        pack(ends(atm), aedge)

        for load in small:
            load.wait()

        def one_hot(shape, test):
            first = lax.broadcasted_iota(jnp.int32, shape, 0)
            second = lax.broadcasted_iota(jnp.int32, shape, 1)
            return test(first, second).astype(F32).astype(BF16)

        def placed(matrix, width, places, inner=1):
            total = None
            for term, offsets in zip(halves(matrix), places):
                def test(k, j):
                    hit = j == k + offsets[0]
                    for offset in offsets[1:]:
                        hit = jnp.logical_or(hit, j == k + offset)
                    return hit

                piece = lax.dot_general(
                    term, one_hot((matrix.shape[inner], width), test),
                    (((inner,), (0,)), ((), ())), preferred_element_type=F32,
                )
                total = piece if total is None else total + piece
            return total

        deep, high = ocean.shape[1], atm.shape[1]
        wide_o, wide_a = omat.shape[1], amat.shape[1]
        square = jnp.concatenate(
            [
                placed(sea_mix[...], wide_o, ((0, 2 * deep), (deep,)))
                + placed(
                    profile[...], wide_o,
                    ((3 * deep, 3 * deep + 2 * chan), (3 * deep + chan,)), 0,
                ),
                jnp.zeros((deep - sea_levels, wide_o), F32),
            ],
            axis=0,
        )
        omat[...] = square.astype(BF16)
        both = jnp.concatenate(
            [
                air_mix[...],
                jnp.dot(
                    response[...], air_mix[...], precision=lax.Precision.HIGHEST,
                    preferred_element_type=F32,
                ),
            ],
            axis=0,
        )
        amat[...] = placed(both, wide_a, ((0, 2 * high), (high,))).astype(BF16)
        field = lax.broadcasted_iota(jnp.int32, (chan, cells_a), 0)
        factors = LINK * jnp.broadcast_to(response[:, last:last + 1], (chan, cells_a))
        for c in range(chan):
            factors = factors + jnp.where(field == c, factor[c], 0.0)
        coef[...] = factors
        wet[...] = sea[...].astype(F32)

        spot = one_hot(
            (rows * chan * per_tile, chan * rows),
            lambda k, j: j == (k // per_tile) % chan * rows + k // (per_tile * chan),
        )
        flux_ref[...] = jnp.dot(
            spot, flux_in[...], preferred_element_type=F32
        ).astype(BF16).reshape(rows, chan * per_tile, cells_a)

        slots = 9 * rows
        offset = offset_in[...]
        step_row = (offset >= 3).astype(jnp.int32) + (offset >= 6).astype(jnp.int32)
        dest_row = reflect(ci + step_row - 1, comp_count)
        dest_col = reflect(li + (offset - 3 * step_row) - 1, lev_count)
        slot = ((dest_row - ci + 1) * 3 + (dest_col - li + 1)) * rows + tile_in[...]
        pick_ref[...] = (
            lax.broadcasted_iota(jnp.int32, (slots, pairs), 0) == slot
        ).astype(F32).astype(BF16)
        group = 16
        owner = one_hot(
            (rows * group, pairs),
            lambda k, q: jnp.logical_and(
                q == k // group * per_tile + k % group, k % group < per_tile
            ),
        )
        wanted[...] = lax.dot_general(
            owner, pick_ref[...], (((1,), (1,)), ((), ())), preferred_element_type=F32
        ).astype(BF16)

        pl.semaphore_wait(barrier, tall * wide - 1)

        for n, (di, dj) in enumerate(NEAR):
            if n != 4:
                @pl.when(there(di, dj))
                def _():
                    surf_copy(n).start()
        start_sides(atm_parts, 0)
        start_sides(ocean_parts, 0)

        which = lax.broadcasted_iota(jnp.int32, (chan * per_tile, cells_a), 0) % per_tile

        def multiply(y, carry):
            load_weight(y).wait()
            flux = flux_ref[y]
            left = jnp.concatenate(
                [jnp.where(which == p, flux, 0.0).astype(BF16) for p in range(per_tile)], axis=1
            )
            out = jnp.dot(left, wbuf[y], preferred_element_type=F32)
            at = pl.ds(pl.multiple_of(y * per_tile, per_tile), per_tile)
            for c in range(chan):
                prod[c, at, :] = out[c * per_tile:(c + 1) * per_tile]
            return carry

        lax.fori_loop(0, rows, multiply, 0)

        pick = jnp.concatenate([pick_ref[...], pick_ref[...]], axis=1)
        for c in range(chan):
            hi, lo = halves(prod[c])
            sums = jnp.dot(
                pick, jnp.concatenate([hi, lo], axis=0), preferred_element_type=F32
            ).astype(BF16)
            for n in range(9):
                part[n, c] = sums[n * rows:(n + 1) * rows]
        for n, (di, dj) in enumerate(NEAR):
            if n != 4:
                @pl.when(there(di, dj))
                def _():
                    part_copy(n).start()

        for n, (di, dj) in enumerate(NEAR):
            if n != 4:
                @pl.when(there(-di, -dj))
                def _():
                    surf_copy(n).wait_recv()
        found = jnp.dot(wanted[...], surf[...].reshape(slots, cells_o), preferred_element_type=F32)
        spare = lax.broadcasted_iota(jnp.int32, (rows * group, cells_o), 0) % group >= per_tile
        gathered[...] = jnp.where(spare, 1.0, found).astype(BF16).reshape(rows, group, cells_o)
        line = lax.broadcasted_iota(jnp.int32, (8, cells_a), 0)

        def regrid(y, carry):
            out = lax.dot_general(
                gathered[y], wbuf[y], (((1,), (1,)), ((), ())), preferred_element_type=F32
            )
            num = jnp.zeros((8, cells_a), F32)
            den = jnp.zeros((8, cells_a), F32)
            for p in range(per_tile):
                cols = slice(p * cells_a, (p + 1) * cells_a)
                num = num + jnp.where(line == p, out[0:8, cols], 0.0)
                den = den + out[8:16, cols]
            total = jnp.sum(num, axis=0, keepdims=True)
            sst[y] = jnp.broadcast_to(total, (8, cells_a)) / den
            return carry

        lax.fori_loop(0, rows, regrid, 0)
        flux_out[...] = jnp.zeros_like(flux_out)

        def stencil(parts, s, r):
            state, rbuf, cbuf = parts[0], parts[1], parts[2]
            depth, width = state.shape[1], state.shape[2]
            lane = lax.broadcasted_iota(jnp.int32, (depth, 128), 1)
            x = state[r]
            up = rbuf[s, 0] if r == 0 else state[r - 1]
            down = rbuf[s, 1] if r == rows - 1 else state[r + 1]
            west = pltpu.roll(x, 1, 1)
            east = pltpu.roll(x, width - 1, 1)
            from_west = cbuf[s, 0]
            if r:
                from_west = pltpu.roll(from_west, 128 - r, 1)
            from_east = pltpu.roll(cbuf[s, 1], 127 - r, 1)
            west_end = jnp.where(lane == 0, from_west, west[:, 0:128])
            east_end = jnp.where(lane == 127, from_east, east[:, width - 128:width])
            if width > 128:
                west_end = jnp.concatenate([west_end, west[:, 128:]], axis=1)
                east_end = jnp.concatenate([east[:, 0:width - 128], east_end], axis=1)
            return (1.0 - 4.0 * RATE) * x + RATE * ((up + down) + (west_end + east_end))

        def turned_back(state, target, levels):
            for r in range(rows):
                for h in range(target.shape[0]):
                    target[h, pl.ds(r, levels, stride=rows), :] = state[
                        r, 0:levels, 128 * h:128 * (h + 1)
                    ]

        def saves(source, target, sem):
            return [
                pltpu.make_async_copy(
                    source.at[h], target.at[:, pl.ds(128 * h, 128)], sem.at[h]
                )
                for h in range(source.shape[0])
            ]

        def step(s, carry):
            def spread_atm(r):
                hi, lo = halves(stencil(atm_parts, s, r))
                au[r] = jnp.concatenate([hi, hi, lo], axis=0)

            wait_sides(atm_parts, s, (2, 3))
            for r in range(1, rows - 1):
                spread_atm(r)
            wait_sides(atm_parts, s, (0, 1))
            spread_atm(0)
            spread_atm(rows - 1)
            wait_sent(atm_parts, s)
            depth = atm.shape[1]
            level = lax.broadcasted_iota(jnp.int32, (depth, cells_a), 0)
            def mix_atm(r):
                mixed = jnp.dot(amat[...], au[r], preferred_element_type=F32)
                gap = sst[r, 0:1] - mixed[last:last + 1]
                flux_out[r] += mixed[last + 1:last + 1 + chan] + coef[...] * gap
                atm[r] = mixed + jnp.where(level == last, LINK * gap, 0.0)

            mix_atm(0)
            mix_atm(rows - 1)

            @pl.when(s < STEPS - 1)
            def _():
                start_sides(atm_parts, s + 1, (0, 1))

            for r in range(1, rows - 1):
                mix_atm(r)

            @pl.when(s < STEPS - 1)
            def _():
                pack(ends(atm), aedge)
                start_sides(atm_parts, s + 1, (2, 3))

            @pl.when(s == STEPS - 1)
            def _():
                turned_back(atm, atm_load, last + 1)
                for save in saves(atm_load, atm_out, al_sem):
                    save.start()

            @pl.when(s == 0)
            def _():
                total = part[4].astype(F32).reshape(chan * rows, cells_o)
                prod[0, 0:chan * rows] = total
                for n, (di, dj) in enumerate(NEAR):
                    if n != 4:
                        @pl.when(there(-di, -dj))
                        def _():
                            part_copy(n).wait_recv()
                            prod[0, 0:chan * rows] += precv[n].astype(F32).reshape(
                                chan * rows, cells_o
                            )
                size = 4 * chan
                to = lax.broadcasted_iota(jnp.int32, (rows * size, chan * rows), 0)
                source = lax.broadcasted_iota(jnp.int32, (rows * size, chan * rows), 1)
                place = to % size
                turn = (
                    jnp.logical_and(
                        source == (place % chan) * rows + to // size, place < 3 * chan
                    )
                ).astype(F32).astype(BF16)
                hi, lo = halves(prod[0, 0:chan * rows])
                laid = jnp.dot(
                    jnp.concatenate([turn, turn], axis=1),
                    jnp.concatenate([hi, lo], axis=0),
                    preferred_element_type=F32,
                )
                high = laid.astype(BF16).astype(F32)
                at = lax.broadcasted_iota(jnp.int32, laid.shape, 0) % size
                both = jnp.where(at < 2 * chan, high, laid - high).astype(BF16)
                both = both.reshape(rows, size, cells_o)
                mixing = 3 * ocean.shape[1]
                for r in range(rows):
                    ou[r, mixing:mixing + size] = both[r]

            def spread_ocean(r):
                hi, lo = halves(stencil(ocean_parts, s, r))
                ou[r, 0:3 * deep] = jnp.concatenate([hi, hi, lo], axis=0)

            def mix_ocean(r):
                ocean[r] = wet[r:r + 1] * jnp.dot(
                    omat[...], ou[r], preferred_element_type=F32
                )

            wait_sides(ocean_parts, s, (2, 3))
            for r in range(1, rows - 1):
                spread_ocean(r)
            wait_sides(ocean_parts, s, (0, 1))
            spread_ocean(0)
            spread_ocean(rows - 1)
            wait_sent(ocean_parts, s)
            mix_ocean(0)
            mix_ocean(rows - 1)

            @pl.when(s < STEPS - 1)
            def _():
                start_sides(ocean_parts, s + 1, (0, 1))

            for r in range(1, rows - 1):
                mix_ocean(r)

            @pl.when(s < STEPS - 1)
            def _():
                pack(ends(ocean), oedge)
                start_sides(ocean_parts, s + 1, (2, 3))

            return carry

        lax.fori_loop(0, STEPS, step, 0)

        turned_back(ocean, ocean_load, sea_levels)
        for save in saves(ocean_load, ocean_out, ol_sem):
            save.start()
        for r in range(rows):
            flux_sum[pl.ds(r, chan, stride=rows), :] = flux_out[r] * (1.0 / STEPS)
        flux_end[...] = flux_sum[...].astype(BF16)
        save_flux = pltpu.make_async_copy(flux_end, flux_far_out, in_sem.at[0])
        save_flux.start()
        for n, (di, dj) in enumerate(NEAR):
            if n != 4:
                @pl.when(there(di, dj))
                def _():
                    surf_copy(n).wait_send()
                    part_copy(n).wait_send()
        save_flux.wait()
        for save in saves(ocean_load, ocean_out, ol_sem) + saves(atm_load, atm_out, al_sem):
            save.wait()

    return kernel


def body(
    atm_state,
    ocean_state,
    flux_prev,
    pair_offset,
    pair_tile,
    pair_weight,
    atm_mix,
    ocean_mix,
    exchange_response_matrix,
    exchange_factor_array,
    depth_profile,
    sea_mask,
):
    comp_count = lax.axis_size("comp")
    lev_count = lax.axis_size("lev")
    pairs, cells_a, cells_o = pair_weight.shape
    air, rows = atm_state.shape[:2]
    sea = ocean_state.shape[0]
    chan = flux_prev.shape[0]
    per_tile = pairs // rows
    deep = (sea + 15) // 16 * 16
    high = (air + chan + 15) // 16 * 16
    dims = (rows, per_tile, chan, cells_a, cells_o, air - 1, sea, (comp_count, lev_count))
    anywhere = pl.BlockSpec(memory_space=pl.ANY)
    dma = pltpu.SemaphoreType.DMA
    atm_end, ocean_end, flux_end = pl.pallas_call(
        make_kernel(dims),
        out_shape=(
            jax.ShapeDtypeStruct((air * rows, cells_a), F32),
            jax.ShapeDtypeStruct((sea * rows, cells_o), F32),
            jax.ShapeDtypeStruct((chan * rows, cells_a), BF16),
        ),
        in_specs=[anywhere] * 12,
        out_specs=(anywhere, anywhere, anywhere),
        scratch_shapes=[
            pltpu.VMEM((rows, chan, cells_a), F32),
            pltpu.VMEM((chan * rows, cells_a), F32),
            pltpu.VMEM((chan * rows, cells_a), BF16),
            pltpu.VMEM((chan * rows, cells_a), BF16),
            pltpu.VMEM((1, pairs), jnp.int32),
            pltpu.VMEM((1, pairs), jnp.int32),
            pltpu.VMEM((air, air), F32),
            pltpu.VMEM((sea, sea), F32),
            pltpu.VMEM((chan, air), F32),
            pltpu.SMEM((chan,), F32),
            pltpu.VMEM((chan, sea), F32),
            pltpu.VMEM((rows, cells_o), jnp.int32),
            pltpu.VMEM((cells_o // 128, sea * rows, 128), F32),
            pltpu.VMEM((cells_a // 128, air * rows, 128), F32),
            pltpu.VMEM((rows, deep, cells_o), F32),
            pltpu.VMEM((rows, high, cells_a), F32),
            pltpu.VMEM((rows, per_tile * cells_a, cells_o), BF16),
            pltpu.VMEM((chan, pairs, cells_o), F32),
            pltpu.VMEM((9, chan, rows, cells_o), BF16),
            pltpu.VMEM((9, chan, rows, cells_o), BF16),
            pltpu.VMEM((9, rows, cells_o), BF16),
            pltpu.VMEM((rows, 16, cells_o), BF16),
            pltpu.VMEM((rows, chan * per_tile, cells_a), BF16),
            pltpu.VMEM((9 * rows, pairs), BF16),
            pltpu.VMEM((rows * 16, 9 * rows), BF16),
            pltpu.VMEM((deep, 3 * deep + 4 * chan), BF16),
            pltpu.VMEM((high, 3 * high), BF16),
            pltpu.VMEM((chan, cells_a), F32),
            pltpu.VMEM((rows, cells_o), F32),
            pltpu.VMEM((rows, 3 * deep + 4 * chan, cells_o), BF16),
            pltpu.VMEM((rows, 3 * high, cells_a), BF16),
            pltpu.VMEM((rows, 8, cells_a), F32),
            pltpu.VMEM((STEPS, 2, deep, cells_o), F32),
            pltpu.VMEM((STEPS, 2, deep, 128), F32),
            pltpu.VMEM((2, deep, 128), F32),
            pltpu.VMEM((STEPS, 2, high, cells_a), F32),
            pltpu.VMEM((STEPS, 2, high, 128), F32),
            pltpu.VMEM((2, high, 128), F32),
            dma((1,)),
            dma((9,)),
            dma((cells_o // 128,)),
            dma((cells_a // 128,)),
            dma((rows,)),
            dma((9,)),
            dma((9,)),
            dma((9,)),
            dma((9,)),
            dma((STEPS, 4)),
            dma((STEPS, 4)),
            dma((STEPS, 4)),
            dma((STEPS, 4)),
        ],
        compiler_params=pltpu.CompilerParams(
            collective_id=0, has_side_effects=True, vmem_limit_bytes=60 * 1024 * 1024
        ),
        name="coupled",
    )(
        atm_state.reshape(air * rows, cells_a),
        ocean_state.reshape(sea * rows, cells_o),
        flux_prev.reshape(chan * rows, cells_a),
        pair_offset.reshape(1, pairs),
        pair_tile.reshape(1, pairs),
        pair_weight.reshape(rows, per_tile * cells_a, cells_o),
        atm_mix, ocean_mix, exchange_response_matrix, exchange_factor_array,
        depth_profile.T, sea_mask,
    )
    return (
        atm_end.reshape(air, rows, cells_a),
        ocean_end.reshape(sea, rows, cells_o),
        flux_end.reshape(chan, rows, cells_a),
    )


def solution(mesh):
    in_specs = (
        P("member", "comp", "lev"),
        P("member", "comp", "lev"),
        P("member", "comp", "lev"),
        P(("comp", "lev")),
        P(("comp", "lev")),
        P(("comp", "lev"), None, None),
        P(),
        P(),
        P(),
        P(),
        P(),
        P("comp", "lev"),
    )
    out_specs = (P("member", "comp", "lev"), P("member", "comp", "lev"), P("member", "comp", "lev"))
    return jax.shard_map(body, mesh=mesh, in_specs=in_specs, out_specs=out_specs, check_vma=False)
```

```python
import jax
import jax.numpy as jnp
from jax import lax
from jax.experimental import pallas as pl
from jax.experimental.pallas import tpu as pltpu
from jax.sharding import PartitionSpec as P

STEPS = 4
RATE = 0.24
LINK = 0.5
BF16 = jnp.bfloat16
F32 = jnp.float32
MESH = pl.DeviceIdType.MESH
NEAR = [(n // 3 - 1, n % 3 - 1) for n in range(9)]
SIDES = [(-1, 0), (1, 0), (0, -1), (0, 1)]


def halves(x):
    hi = x.astype(BF16)
    return hi, (x - hi.astype(F32)).astype(BF16)


def reflect(index, count):
    return jnp.where(
        index < 0, -index, jnp.where(index > count - 1, 2 * (count - 1) - index, index)
    )


def make_kernel(dims):
    rows, per_tile, chan, cells_a, cells_o, last, sea_levels, counts = dims
    pairs = rows * per_tile

    def kernel(
        atm_in, ocean_in, flux_far, offset_far, tile_far, weight_in, air_far, sea_far,
        response_far, factor_far, profile_far, mask_far,
        atm_out, ocean_out, flux_far_out,
        flux_out, flux_sum, flux_end, flux_in, offset_in, tile_in, air_mix, sea_mix, response, factor, profile, sea,
        ocean_load, atm_load, ocean, atm, wbuf, prod, part, precv, surf, gathered, flux_ref,
        pick_ref, wanted, omat, amat, coef, wet, ou, au, sst,
        orow, ocol, oedge, arow, acol, aedge,
        in_sem, small_sem, ol_sem, al_sem, w_sem, surf_send, surf_recv, part_send, part_recv,
        o_send, o_recv, a_send, a_recv,
    ):
        ci = lax.axis_index("comp")
        li = lax.axis_index("lev")
        comp_count, lev_count = counts

        def there(di, dj):
            ok = None
            for delta, index, count in ((di, ci, comp_count), (dj, li, lev_count)):
                if delta == -1:
                    one = index > 0
                elif delta == 1:
                    one = index < count - 1
                else:
                    continue
                ok = one if ok is None else jnp.logical_and(ok, one)
            return ok

        def device(di, dj):
            return {
                "comp": jnp.clip(ci + di, 0, comp_count - 1),
                "lev": jnp.clip(li + dj, 0, lev_count - 1),
            }

        loads = [
            pltpu.make_async_copy(
                source.at[:, pl.ds(128 * h, 128)], target.at[h], sem.at[h]
            )
            for source, target, sem in (
                (ocean_in, ocean_load, ol_sem), (atm_in, atm_load, al_sem)
            )
            for h in range(target.shape[0])
        ]
        for load in loads:
            load.start()
        small = [
            pltpu.make_async_copy(source, target, small_sem.at[k])
            for k, (source, target) in enumerate((
                (flux_far, flux_in), (offset_far, offset_in), (tile_far, tile_in),
                (air_far, air_mix), (sea_far, sea_mix), (response_far, response),
                (factor_far, factor), (profile_far, profile), (mask_far, sea),
            ))
        ]
        for load in small:
            load.start()

        def load_weight(y):
            return pltpu.make_async_copy(weight_in.at[y], wbuf.at[y], w_sem.at[y])

        def start_weight(y, carry):
            load_weight(y).start()
            return carry

        lax.fori_loop(0, rows, start_weight, 0)

        for n, (di, dj) in enumerate(NEAR):
            if n != 4:
                @pl.when(jnp.logical_not(there(di, dj)))
                def _():
                    surf[n] = jnp.zeros(surf.shape[1:], BF16)
        for side, (di, dj) in enumerate(SIDES):
            @pl.when(jnp.logical_not(there(di, dj)))
            def _():
                for rbuf, cbuf in ((orow, ocol), (arow, acol)):
                    buf = rbuf if side < 2 else cbuf
                    for s in range(STEPS):
                        buf[s, side % 2] = jnp.zeros(buf.shape[2:], F32)

        barrier = pltpu.get_barrier_semaphore()
        for n, (di, dj) in enumerate(NEAR):
            if n != 4:
                @pl.when(there(di, dj))
                def _():
                    pl.semaphore_signal(
                        barrier, inc=1, device_id=device(di, dj), device_id_type=MESH
                    )
        tall = 1 + (ci > 0).astype(jnp.int32) + (ci < comp_count - 1).astype(jnp.int32)
        wide = 1 + (li > 0).astype(jnp.int32) + (li < lev_count - 1).astype(jnp.int32)

        def remote(src, dst, send, recv, di, dj):
            return pltpu.make_async_remote_copy(
                src_ref=src, dst_ref=dst, send_sem=send, recv_sem=recv,
                device_id=device(di, dj), device_id_type=MESH,
            )

        def surf_copy(n):
            return remote(
                surf.at[4], surf.at[8 - n], surf_send.at[n], surf_recv.at[n], *NEAR[n]
            )

        def part_copy(n):
            return remote(
                part.at[n], precv.at[n], part_send.at[n], part_recv.at[n], *NEAR[n]
            )

        def side_copy(state, rbuf, cbuf, edge, send, recv, s, side):
            if side < 2:
                src = state.at[0 if side == 0 else rows - 1]
                dst = rbuf.at[s, 1 - side]
            else:
                src = edge.at[side - 2]
                dst = cbuf.at[s, 3 - side]
            return remote(
                src, dst, send.at[s, side], recv.at[s, side], *SIDES[side]
            )

        ocean_parts = (ocean, orow, ocol, oedge, o_send, o_recv)
        atm_parts = (atm, arow, acol, aedge, a_send, a_recv)

        def start_sides(parts, s, sides=(0, 1, 2, 3)):
            for side in sides:
                di, dj = SIDES[side]

                @pl.when(there(di, dj))
                def _():
                    side_copy(*parts, s, side).start()

        def wait_sent(parts, s):
            for side, (di, dj) in enumerate(SIDES):
                @pl.when(there(di, dj))
                def _():
                    side_copy(*parts, s, side).wait_send()

        def wait_sides(parts, s, sides):
            for side in sides:
                di, dj = SIDES[side]

                @pl.when(there(-di, -dj))
                def _():
                    side_copy(*parts, s, side).wait_recv()

        def pack(slabs, edge):
            depth = edge.shape[1]
            lane = lax.broadcasted_iota(jnp.int32, (depth, 128), 1)
            left = jnp.zeros((depth, 128), F32)
            right = jnp.zeros((depth, 128), F32)
            for r in range(rows):
                first, final = slabs(r)
                left = jnp.where(lane == r, pltpu.roll(first, r, 1) if r else first, left)
                right = jnp.where(lane == r, pltpu.roll(final, r + 1, 1), right)
            edge[0] = left
            edge[1] = right

        def ends(state):
            width = state.shape[2]
            return lambda r: (state[r, :, 0:128], state[r, :, width - 128:width])

        def turned(source, state, levels):
            depth, width = state.shape[1:]
            for r in range(rows):
                for col in range(0, width, 128):
                    state[r, 0:levels, col:col + 128] = source[
                        col // 128, pl.ds(r, levels, stride=rows), :
                    ]
                if depth > levels:
                    state[r, levels:depth] = jnp.zeros((depth - levels, width), F32)

        for load in loads[:ocean_load.shape[0]]:
            load.wait()
        turned(ocean_load, ocean, sea_levels)
        for h in range(ocean_load.shape[0]):
            surf[4, :, 128 * h:128 * (h + 1)] = ocean_load[h, 0:rows].astype(BF16)
        pack(ends(ocean), oedge)
        for load in loads[ocean_load.shape[0]:]:
            load.wait()
        turned(atm_load, atm, last + 1)
        pack(ends(atm), aedge)

        for load in small:
            load.wait()

        def one_hot(shape, test):
            first = lax.broadcasted_iota(jnp.int32, shape, 0)
            second = lax.broadcasted_iota(jnp.int32, shape, 1)
            return test(first, second).astype(F32).astype(BF16)

        def placed(matrix, width, places, inner=1):
            total = None
            for term, offsets in zip(halves(matrix), places):
                def test(k, j):
                    hit = j == k + offsets[0]
                    for offset in offsets[1:]:
                        hit = jnp.logical_or(hit, j == k + offset)
                    return hit

                piece = lax.dot_general(
                    term, one_hot((matrix.shape[inner], width), test),
                    (((inner,), (0,)), ((), ())), preferred_element_type=F32,
                )
                total = piece if total is None else total + piece
            return total

        deep, high = ocean.shape[1], atm.shape[1]
        wide_o, wide_a = omat.shape[1], amat.shape[1]
        square = jnp.concatenate(
            [
                placed(sea_mix[...], wide_o, ((0, 2 * deep), (deep,)))
                + placed(
                    profile[...], wide_o,
                    ((3 * deep, 3 * deep + 2 * chan), (3 * deep + chan,)), 0,
                ),
                jnp.zeros((deep - sea_levels, wide_o), F32),
            ],
            axis=0,
        )
        omat[...] = square.astype(BF16)
        both = jnp.concatenate(
            [
                air_mix[...],
                jnp.dot(
                    response[...], air_mix[...], precision=lax.Precision.HIGHEST,
                    preferred_element_type=F32,
                ),
            ],
            axis=0,
        )
        amat[...] = placed(both, wide_a, ((0, 2 * high), (high,))).astype(BF16)
        field = lax.broadcasted_iota(jnp.int32, (chan, cells_a), 0)
        factors = LINK * jnp.broadcast_to(response[:, last:last + 1], (chan, cells_a))
        for c in range(chan):
            factors = factors + jnp.where(field == c, factor[c], 0.0)
        coef[...] = factors
        wet[...] = sea[...].astype(F32)

        spot = one_hot(
            (rows * chan * per_tile, chan * rows),
            lambda k, j: j == (k // per_tile) % chan * rows + k // (per_tile * chan),
        )
        flux_ref[...] = jnp.dot(
            spot, flux_in[...], preferred_element_type=F32
        ).astype(BF16).reshape(rows, chan * per_tile, cells_a)

        slots = 9 * rows
        offset = offset_in[...]
        step_row = (offset >= 3).astype(jnp.int32) + (offset >= 6).astype(jnp.int32)
        dest_row = reflect(ci + step_row - 1, comp_count)
        dest_col = reflect(li + (offset - 3 * step_row) - 1, lev_count)
        slot = ((dest_row - ci + 1) * 3 + (dest_col - li + 1)) * rows + tile_in[...]
        pick_ref[...] = (
            lax.broadcasted_iota(jnp.int32, (slots, pairs), 0) == slot
        ).astype(F32).astype(BF16)
        group = 16
        owner = one_hot(
            (rows * group, pairs),
            lambda k, q: jnp.logical_and(
                q == k // group * per_tile + k % group, k % group < per_tile
            ),
        )
        wanted[...] = lax.dot_general(
            owner, pick_ref[...], (((1,), (1,)), ((), ())), preferred_element_type=F32
        ).astype(BF16)

        pl.semaphore_wait(barrier, tall * wide - 1)

        for n, (di, dj) in enumerate(NEAR):
            if n != 4:
                @pl.when(there(di, dj))
                def _():
                    surf_copy(n).start()
        start_sides(atm_parts, 0)
        start_sides(ocean_parts, 0)

        which = lax.broadcasted_iota(jnp.int32, (chan * per_tile, cells_a), 0) % per_tile

        def multiply(y, carry):
            load_weight(y).wait()
            flux = flux_ref[y]
            left = jnp.concatenate(
                [jnp.where(which == p, flux, 0.0).astype(BF16) for p in range(per_tile)], axis=1
            )
            out = jnp.dot(left, wbuf[y], preferred_element_type=F32)
            at = pl.ds(pl.multiple_of(y * per_tile, per_tile), per_tile)
            for c in range(chan):
                prod[c, at, :] = out[c * per_tile:(c + 1) * per_tile]
            return carry

        lax.fori_loop(0, rows, multiply, 0, unroll=2)

        pick = jnp.concatenate([pick_ref[...], pick_ref[...]], axis=1)
        for c in range(chan):
            hi, lo = halves(prod[c])
            sums = jnp.dot(
                pick, jnp.concatenate([hi, lo], axis=0), preferred_element_type=F32
            ).astype(BF16)
            for n in range(9):
                part[n, c] = sums[n * rows:(n + 1) * rows]
        for n, (di, dj) in enumerate(NEAR):
            if n != 4:
                @pl.when(there(di, dj))
                def _():
                    part_copy(n).start()

        for n, (di, dj) in enumerate(NEAR):
            if n != 4:
                @pl.when(there(-di, -dj))
                def _():
                    surf_copy(n).wait_recv()
        found = jnp.dot(wanted[...], surf[...].reshape(slots, cells_o), preferred_element_type=F32)
        spare = lax.broadcasted_iota(jnp.int32, (rows * group, cells_o), 0) % group >= per_tile
        gathered[...] = jnp.where(spare, 1.0, found).astype(BF16).reshape(rows, group, cells_o)
        line = lax.broadcasted_iota(jnp.int32, (8, cells_a), 0)

        def regrid(y, carry):
            out = lax.dot_general(
                gathered[y], wbuf[y], (((1,), (1,)), ((), ())), preferred_element_type=F32
            )
            num = jnp.zeros((8, cells_a), F32)
            den = jnp.zeros((8, cells_a), F32)
            for p in range(per_tile):
                cols = slice(p * cells_a, (p + 1) * cells_a)
                num = num + jnp.where(line == p, out[0:8, cols], 0.0)
                den = den + out[8:16, cols]
            total = jnp.sum(num, axis=0, keepdims=True)
            sst[y] = jnp.broadcast_to(total, (8, cells_a)) / den
            return carry

        lax.fori_loop(0, rows, regrid, 0, unroll=4)
        flux_out[...] = jnp.zeros_like(flux_out)

        def stencil(parts, s, r):
            state, rbuf, cbuf = parts[0], parts[1], parts[2]
            depth, width = state.shape[1], state.shape[2]
            lane = lax.broadcasted_iota(jnp.int32, (depth, 128), 1)
            x = state[r]
            up = rbuf[s, 0] if r == 0 else state[r - 1]
            down = rbuf[s, 1] if r == rows - 1 else state[r + 1]
            west = pltpu.roll(x, 1, 1)
            east = pltpu.roll(x, width - 1, 1)
            from_west = cbuf[s, 0]
            if r:
                from_west = pltpu.roll(from_west, 128 - r, 1)
            from_east = pltpu.roll(cbuf[s, 1], 127 - r, 1)
            west_end = jnp.where(lane == 0, from_west, west[:, 0:128])
            east_end = jnp.where(lane == 127, from_east, east[:, width - 128:width])
            if width > 128:
                west_end = jnp.concatenate([west_end, west[:, 128:]], axis=1)
                east_end = jnp.concatenate([east[:, 0:width - 128], east_end], axis=1)
            return (1.0 - 4.0 * RATE) * x + RATE * ((up + down) + (west_end + east_end))

        def turned_back(state, target, levels):
            for r in range(rows):
                for h in range(target.shape[0]):
                    target[h, pl.ds(r, levels, stride=rows), :] = state[
                        r, 0:levels, 128 * h:128 * (h + 1)
                    ]

        def saves(source, target, sem):
            return [
                pltpu.make_async_copy(
                    source.at[h], target.at[:, pl.ds(128 * h, 128)], sem.at[h]
                )
                for h in range(source.shape[0])
            ]

        def step(s, carry):
            def spread_atm(r):
                hi, lo = halves(stencil(atm_parts, s, r))
                au[r] = jnp.concatenate([hi, hi, lo], axis=0)

            wait_sides(atm_parts, s, (2, 3))
            for r in range(1, rows - 1):
                spread_atm(r)
            wait_sides(atm_parts, s, (0, 1))
            spread_atm(0)
            spread_atm(rows - 1)
            wait_sent(atm_parts, s)
            depth = atm.shape[1]
            level = lax.broadcasted_iota(jnp.int32, (depth, cells_a), 0)
            def mix_atm(r):
                mixed = jnp.dot(amat[...], au[r], preferred_element_type=F32)
                gap = sst[r, 0:1] - mixed[last:last + 1]
                flux_out[r] += mixed[last + 1:last + 1 + chan] + coef[...] * gap
                atm[r] = mixed + jnp.where(level == last, LINK * gap, 0.0)

            mix_atm(0)
            mix_atm(rows - 1)

            @pl.when(s < STEPS - 1)
            def _():
                start_sides(atm_parts, s + 1, (0, 1))

            for r in range(1, rows - 1):
                mix_atm(r)

            @pl.when(s < STEPS - 1)
            def _():
                pack(ends(atm), aedge)
                start_sides(atm_parts, s + 1, (2, 3))

            @pl.when(s == STEPS - 1)
            def _():
                turned_back(atm, atm_load, last + 1)
                for save in saves(atm_load, atm_out, al_sem):
                    save.start()

            @pl.when(s == 0)
            def _():
                total = part[4].astype(F32).reshape(chan * rows, cells_o)
                prod[0, 0:chan * rows] = total
                for n, (di, dj) in enumerate(NEAR):
                    if n != 4:
                        @pl.when(there(-di, -dj))
                        def _():
                            part_copy(n).wait_recv()
                            prod[0, 0:chan * rows] += precv[n].astype(F32).reshape(
                                chan * rows, cells_o
                            )
                size = 4 * chan
                to = lax.broadcasted_iota(jnp.int32, (rows * size, chan * rows), 0)
                source = lax.broadcasted_iota(jnp.int32, (rows * size, chan * rows), 1)
                place = to % size
                turn = (
                    jnp.logical_and(
                        source == (place % chan) * rows + to // size, place < 3 * chan
                    )
                ).astype(F32).astype(BF16)
                hi, lo = halves(prod[0, 0:chan * rows])
                laid = jnp.dot(
                    jnp.concatenate([turn, turn], axis=1),
                    jnp.concatenate([hi, lo], axis=0),
                    preferred_element_type=F32,
                )
                high = laid.astype(BF16).astype(F32)
                at = lax.broadcasted_iota(jnp.int32, laid.shape, 0) % size
                both = jnp.where(at < 2 * chan, high, laid - high).astype(BF16)
                both = both.reshape(rows, size, cells_o)
                mixing = 3 * ocean.shape[1]
                for r in range(rows):
                    ou[r, mixing:mixing + size] = both[r]

            def spread_ocean(r):
                hi, lo = halves(stencil(ocean_parts, s, r))
                ou[r, 0:3 * deep] = jnp.concatenate([hi, hi, lo], axis=0)

            def mix_ocean(r):
                ocean[r] = wet[r:r + 1] * jnp.dot(
                    omat[...], ou[r], preferred_element_type=F32
                )

            wait_sides(ocean_parts, s, (2, 3))
            for r in range(1, rows - 1):
                spread_ocean(r)
            wait_sides(ocean_parts, s, (0, 1))
            spread_ocean(0)
            spread_ocean(rows - 1)
            wait_sent(ocean_parts, s)
            mix_ocean(0)
            mix_ocean(rows - 1)

            @pl.when(s < STEPS - 1)
            def _():
                start_sides(ocean_parts, s + 1, (0, 1))

            for r in range(1, rows - 1):
                mix_ocean(r)

            @pl.when(s < STEPS - 1)
            def _():
                pack(ends(ocean), oedge)
                start_sides(ocean_parts, s + 1, (2, 3))

            return carry

        lax.fori_loop(0, STEPS, step, 0)

        turned_back(ocean, ocean_load, sea_levels)
        for save in saves(ocean_load, ocean_out, ol_sem):
            save.start()
        for r in range(rows):
            flux_sum[pl.ds(r, chan, stride=rows), :] = flux_out[r] * (1.0 / STEPS)
        flux_end[...] = flux_sum[...].astype(BF16)
        save_flux = pltpu.make_async_copy(flux_end, flux_far_out, in_sem.at[0])
        save_flux.start()
        for n, (di, dj) in enumerate(NEAR):
            if n != 4:
                @pl.when(there(di, dj))
                def _():
                    surf_copy(n).wait_send()
                    part_copy(n).wait_send()
        save_flux.wait()
        for save in saves(ocean_load, ocean_out, ol_sem) + saves(atm_load, atm_out, al_sem):
            save.wait()

    return kernel


def body(
    atm_state,
    ocean_state,
    flux_prev,
    pair_offset,
    pair_tile,
    pair_weight,
    atm_mix,
    ocean_mix,
    exchange_response_matrix,
    exchange_factor_array,
    depth_profile,
    sea_mask,
):
    comp_count = lax.axis_size("comp")
    lev_count = lax.axis_size("lev")
    pairs, cells_a, cells_o = pair_weight.shape
    air, rows = atm_state.shape[:2]
    sea = ocean_state.shape[0]
    chan = flux_prev.shape[0]
    per_tile = pairs // rows
    deep = (sea + 15) // 16 * 16
    high = (air + chan + 15) // 16 * 16
    dims = (rows, per_tile, chan, cells_a, cells_o, air - 1, sea, (comp_count, lev_count))
    anywhere = pl.BlockSpec(memory_space=pl.ANY)
    dma = pltpu.SemaphoreType.DMA
    atm_end, ocean_end, flux_end = pl.pallas_call(
        make_kernel(dims),
        out_shape=(
            jax.ShapeDtypeStruct((air * rows, cells_a), F32),
            jax.ShapeDtypeStruct((sea * rows, cells_o), F32),
            jax.ShapeDtypeStruct((chan * rows, cells_a), BF16),
        ),
        in_specs=[anywhere] * 12,
        out_specs=(anywhere, anywhere, anywhere),
        scratch_shapes=[
            pltpu.VMEM((rows, chan, cells_a), F32),
            pltpu.VMEM((chan * rows, cells_a), F32),
            pltpu.VMEM((chan * rows, cells_a), BF16),
            pltpu.VMEM((chan * rows, cells_a), BF16),
            pltpu.VMEM((1, pairs), jnp.int32),
            pltpu.VMEM((1, pairs), jnp.int32),
            pltpu.VMEM((air, air), F32),
            pltpu.VMEM((sea, sea), F32),
            pltpu.VMEM((chan, air), F32),
            pltpu.SMEM((chan,), F32),
            pltpu.VMEM((chan, sea), F32),
            pltpu.VMEM((rows, cells_o), jnp.int32),
            pltpu.VMEM((cells_o // 128, sea * rows, 128), F32),
            pltpu.VMEM((cells_a // 128, air * rows, 128), F32),
            pltpu.VMEM((rows, deep, cells_o), F32),
            pltpu.VMEM((rows, high, cells_a), F32),
            pltpu.VMEM((rows, per_tile * cells_a, cells_o), BF16),
            pltpu.VMEM((chan, pairs, cells_o), F32),
            pltpu.VMEM((9, chan, rows, cells_o), BF16),
            pltpu.VMEM((9, chan, rows, cells_o), BF16),
            pltpu.VMEM((9, rows, cells_o), BF16),
            pltpu.VMEM((rows, 16, cells_o), BF16),
            pltpu.VMEM((rows, chan * per_tile, cells_a), BF16),
            pltpu.VMEM((9 * rows, pairs), BF16),
            pltpu.VMEM((rows * 16, 9 * rows), BF16),
            pltpu.VMEM((deep, 3 * deep + 4 * chan), BF16),
            pltpu.VMEM((high, 3 * high), BF16),
            pltpu.VMEM((chan, cells_a), F32),
            pltpu.VMEM((rows, cells_o), F32),
            pltpu.VMEM((rows, 3 * deep + 4 * chan, cells_o), BF16),
            pltpu.VMEM((rows, 3 * high, cells_a), BF16),
            pltpu.VMEM((rows, 8, cells_a), F32),
            pltpu.VMEM((STEPS, 2, deep, cells_o), F32),
            pltpu.VMEM((STEPS, 2, deep, 128), F32),
            pltpu.VMEM((2, deep, 128), F32),
            pltpu.VMEM((STEPS, 2, high, cells_a), F32),
            pltpu.VMEM((STEPS, 2, high, 128), F32),
            pltpu.VMEM((2, high, 128), F32),
            dma((1,)),
            dma((9,)),
            dma((cells_o // 128,)),
            dma((cells_a // 128,)),
            dma((rows,)),
            dma((9,)),
            dma((9,)),
            dma((9,)),
            dma((9,)),
            dma((STEPS, 4)),
            dma((STEPS, 4)),
            dma((STEPS, 4)),
            dma((STEPS, 4)),
        ],
        compiler_params=pltpu.CompilerParams(
            collective_id=0, has_side_effects=True, vmem_limit_bytes=60 * 1024 * 1024
        ),
        name="coupled",
    )(
        atm_state.reshape(air * rows, cells_a),
        ocean_state.reshape(sea * rows, cells_o),
        flux_prev.reshape(chan * rows, cells_a),
        pair_offset.reshape(1, pairs),
        pair_tile.reshape(1, pairs),
        pair_weight.reshape(rows, per_tile * cells_a, cells_o),
        atm_mix, ocean_mix, exchange_response_matrix, exchange_factor_array,
        depth_profile.T, sea_mask,
    )
    return (
        atm_end.reshape(air, rows, cells_a),
        ocean_end.reshape(sea, rows, cells_o),
        flux_end.reshape(chan, rows, cells_a),
    )


def solution(mesh):
    in_specs = (
        P("member", "comp", "lev"),
        P("member", "comp", "lev"),
        P("member", "comp", "lev"),
        P(("comp", "lev")),
        P(("comp", "lev")),
        P(("comp", "lev"), None, None),
        P(),
        P(),
        P(),
        P(),
        P(),
        P("comp", "lev"),
    )
    out_specs = (P("member", "comp", "lev"), P("member", "comp", "lev"), P("member", "comp", "lev"))
    return jax.shard_map(body, mesh=mesh, in_specs=in_specs, out_specs=out_specs, check_vma=False)
```
